512 devices in a mesh: sensor: 64 (over z, y), slot: 4 (over x_hi, core), day: 2 (over x_lo).
Axes of the slice: x: 4 (x_hi: 2, x_lo: 2; x = x_hi * 2 + x_lo), y: 4, z: 16, core: 2. Of those that a mesh axis runs over, the one named last changes fastest.
Arguments:
- traffic: float32 [10, 288, 204800], P('day', 'slot', 'sensor'), may hold values from -1400 to 1400
- slot_factor: float32 [288, 128], replicated, may hold values from -6 to 6
- day_factor: float32 [10, 128], replicated, may hold values from -6 to 6
Outputs:
- sensor_factor: float32 [204800, 128], P(('sensor', 'slot', 'day'))
- slot_factor_new: float32 [288, 128], P('slot')
- day_factor_new: float32 [10, 128], P('day')
The draws below stay inside these ranges and needn't reach their ends.
All inputs are finite; a program needn't handle non-finite values.
Results may differ from the reference program's by a relative error of at most 0.0003.
Values sent between devices are 32-bit elements; how exact they have to be, the bound alone decides.
A program may use at most 64 MiB of HBM per device.

```python
import math
import jax
import jax.numpy as jnp
from jax import lax

R = 128
SEN_DEV = 3200
SLOTS = 288
DAYS = 10
SENSORS = 204800


def draw_traffic(key, part):
    key = jax.random.fold_in(key, 7)
    sensor_key, slot_key, noise_key = jax.random.split(key, 3)
    sensor_place = jnp.arange(SENSORS, dtype=jnp.float32) / SENSORS
    slot_place = jnp.arange(SLOTS, dtype=jnp.float32) / SLOTS
    sensor_top = 10.0
    slot_top = 10.0
    offset = 0.5
    noise = jnp.clip(jax.random.normal(noise_key, (DAYS, SLOTS, SENSORS), jnp.float32), -4.0, 4.0)
    sensor_scale = jnp.exp(jax.random.uniform(sensor_key, (SENSORS,), jnp.float32, 0.0, math.log(sensor_top)))
    sensor_scale = sensor_scale * (1.0 + 0.75 * sensor_place)
    slot_scale = jnp.exp(jax.random.uniform(slot_key, (SLOTS,), jnp.float32, 0.0, math.log(slot_top)))
    slot_scale = slot_scale * (1.0 + 0.75 * slot_place)
    return slot_scale[None, :, None] * sensor_scale[None, None, :] * (offset + noise)


def bell_draw(rng, shape, scale, limit, kind=jnp.bfloat16):
    values = scale * jax.random.normal(rng, shape, jnp.float32)
    return jnp.clip(values, min=-limit, max=limit).astype(kind)


def setup_inputs(seed: int = 0) -> dict:
    keys = jax.random.split(jax.random.key(seed), 4)
    traffic = draw_traffic(jax.random.fold_in(keys[3], 71), 0)
    slot_factor = bell_draw(keys[1], (SLOTS, R), 1.0, 6.0, jnp.float32)
    day_factor = bell_draw(keys[2], (DAYS, R), 1.0, 6.0, jnp.float32)
    return {"traffic": traffic, "slot_factor": slot_factor, "day_factor": day_factor}


highest = lax.Precision.HIGHEST
ridge_scale = 0.001
epsilon = 1e-05

def gram_of(factor_rows):
    return jnp.einsum('ir,is->rs', factor_rows, factor_rows, precision=highest)

def regularize(matrix):
    order_count = matrix.shape[0]
    diag_mean = jnp.mean(jnp.diagonal(matrix))
    return matrix + ridge_scale * diag_mean * jnp.eye(order_count, dtype=matrix.dtype)

def solve_rows(right_side, normal_matrix):
    lower_factor = jnp.linalg.cholesky(normal_matrix)
    halfway = lax.linalg.triangular_solve(lower_factor, right_side, left_side=False, lower=True, transpose_a=True)
    return lax.linalg.triangular_solve(lower_factor, halfway, left_side=False, lower=True, transpose_a=False)

def normalize(raw_gram, row_count):
    norms = jnp.sqrt(jnp.diagonal(raw_gram) / row_count + epsilon)
    return (norms, raw_gram / (norms[:, None] * norms[None, :]))

def reference(traffic, slot_factor, day_factor):
    gram_slot = gram_of(slot_factor)
    gram_day = gram_of(day_factor)
    normal_sensor = regularize(gram_slot * gram_day)
    block_count = SENSORS // SEN_DEV

    def mode_one(index):
        segment = lax.dynamic_slice_in_dim(traffic, index * SEN_DEV, SEN_DEV, 2)
        partial_value = jnp.einsum('kji,jr->kir', segment, slot_factor, precision=highest)
        return jnp.einsum('kir,kr->ir', partial_value, day_factor, precision=highest)
    sensor_rhs = lax.map(mode_one, jnp.arange(block_count, dtype=jnp.int32)).reshape(SENSORS, R)
    sensor_raw = solve_rows(sensor_rhs, normal_sensor)
    sensor_norms, gram_sensor = normalize(gram_of(sensor_raw), SENSORS)
    sensor_factor = sensor_raw / sensor_norms[None, :]

    def mode_two(total, index):
        segment = lax.dynamic_slice_in_dim(traffic, index * SEN_DEV, SEN_DEV, 2)
        factor_rows = lax.dynamic_slice_in_dim(sensor_factor, index * SEN_DEV, SEN_DEV, 0)
        return (total + jnp.einsum('kji,ir->kjr', segment, factor_rows, precision=highest), None)
    start_total = jnp.zeros((DAYS, SLOTS, R), jnp.float32)
    contracted, unused = lax.scan(mode_two, start_total, jnp.arange(block_count, dtype=jnp.int32))
    slot_rhs = lax.optimization_barrier(jnp.sum(contracted * day_factor[:, None, :], axis=0))
    slot_raw = solve_rows(slot_rhs, regularize(gram_sensor * gram_day))
    slot_norms, gram_slot_new = normalize(gram_of(slot_raw), SLOTS)
    slot_factor_new = slot_raw / slot_norms[None, :]
    day_rhs = lax.optimization_barrier(jnp.sum(contracted * slot_factor_new[None, :, :], axis=1))
    day_factor_new = solve_rows(day_rhs, regularize(gram_sensor * gram_slot_new))
    return (sensor_factor, slot_factor_new, day_factor_new)
```

```python
import jax
import jax.numpy as jnp
from jax import lax
from jax.experimental import pallas as pl
from jax.experimental.pallas import tpu as pltpu
from jax.sharding import PartitionSpec as P

MESH = pl.DeviceIdType.MESH
highest = lax.Precision.HIGHEST
f32 = jnp.float32
bf16 = jnp.bfloat16
ridge_scale = 0.001
epsilon = 1e-05

R = 128
NX, NY, NZ = 4, 4, 16
GROUP = 8
WINDOW, STRIDE, SHIFT = 512, 384, 16
SLOT_PIECE = 16


def dot(a, b, contract=((1,), (0,)), precision=None):
    return lax.dot_general(a, b, (contract, ((), ())), precision=precision, preferred_element_type=f32)


def gram_of(rows):
    return dot(rows, rows, ((0,), (0,)), highest)


def diagonal_mask():
    return lax.broadcasted_iota(jnp.int32, (R, R), 0) == lax.broadcasted_iota(jnp.int32, (R, R), 1)


def regularize(matrix):
    eye = diagonal_mask()
    mean = jnp.sum(jnp.where(eye, matrix, 0.0)) / R
    return matrix + jnp.where(eye, ridge_scale * mean, 0.0)


def inverse(matrix):
    lane = lax.broadcasted_iota(jnp.int32, (8, R), 1)
    sub = lax.broadcasted_iota(jnp.int32, (8, R), 0)
    lane_rest = lax.broadcasted_iota(jnp.int32, (R - 8, R), 1)

    def step(_, matrix):
        top, rest = matrix[0:8], matrix[8:]
        rows = [jnp.broadcast_to(top[i : i + 1, :], (8, R)) for i in range(8)]
        a = {(i, j): jnp.broadcast_to(rows[i][:, j : j + 1], (8, R)) for i in range(8) for j in range(i, 8)}
        rows = [jnp.where(lane == i, 1.0, jnp.where(lane < 8, 0.0, rows[i])) for i in range(8)]
        lower, scale = {}, []
        for t in range(8):
            scale.append(1.0 / a[t, t])
            for s in range(t + 1, 8):
                lower[s, t] = a[t, s] * scale[t]
            for s in range(t + 1, 8):
                for u in range(s, 8):
                    a[s, u] = a[s, u] - lower[s, t] * a[t, u]
                rows[s] = rows[s] - lower[s, t] * rows[t]
        rows = [rows[t] * scale[t] for t in range(8)]
        for t in range(7, -1, -1):
            for s in range(t):
                rows[s] = rows[s] - lower[t, s] * rows[t]
        new_top = rows[7]
        for i in range(7):
            new_top = jnp.where(sub == i, rows[i], new_top)
        base = jnp.where(lane_rest < 8, 0.0, rest)
        for i in range(8):
            base = base - rest[:, i : i + 1] * rows[i][0:1, :]
        return pltpu.roll(jnp.concatenate([base, new_top], axis=0), R - 8, 1)

    return lax.fori_loop(0, R // 8, step, matrix)


def split(value):
    high = value.astype(bf16)
    return high, (value - high.astype(f32)).astype(bf16)


class Exchange:
    def __init__(self, refs, count, me, device, source=None):
        self.buffer, self.send_sem, self.recv_sem = refs
        self.count, self.me, self.device, self.source = count, me, device, source

    def copy(self, k, slot):
        peer = lax.rem(self.me + k, self.count)
        source = self.buffer.at[self.me] if self.source is None else self.source.at[peer]
        return pltpu.make_async_remote_copy(
            src_ref=source,
            dst_ref=self.buffer.at[self.me if slot is None else peer],
            send_sem=self.send_sem.at[k],
            recv_sem=self.recv_sem.at[self.me if slot is None else peer],
            device_id=self.device(peer),
            device_id_type=MESH,
        )

    def each(self, act):
        def step(i, carry):
            act(lax.rem(i + self.count // 2 - 1, self.count - 1) + 1)
            return carry

        lax.fori_loop(0, self.count - 1, step, 0)

    def start(self):
        self.each(lambda k: self.copy(k, None).start())

    def wait_recv(self):
        self.each(lambda k: self.copy(k, "peer").wait_recv())

    def wait_send(self):
        self.each(lambda k: self.copy(k, None).wait_send())

    def total(self):
        total = self.buffer[0]
        for i in range(1, self.count):
            total = total + self.buffer[i]
        return total


def body(
    sensor_count, slot_count,
    traffic, slot_ref, day_ref, sensor_out, slot_out, day_out,
    t_all, t_high, t_low, w_cat, load_sem,
    win_sib, win_own, sib_recv, sib_ssem, sib_rsem, x_send, x_recv, x_ssem, x_rsem,
    gathered, gat_ssem, gat_rsem, fwd_ssem, fwd_rsem,
    c_wide, c_low,
    gram_part, gx_buf, gx_s, gx_r, gy_buf, gy_s, gy_r, gz_buf, gz_s, gz_r, ga_buf, ga_s, ga_r,
    slot_part, s8_buf, s8_s, s8_r, sz_buf, sz_s, sz_r, sa_buf, sa_s, sa_r, sx_buf, sx_s, sx_r,
    dy_buf, dy_s, dy_r, dz_buf, dz_s, dz_r,
):
    days, slots, sensors = traffic.shape
    rows = days * slots
    padded = t_all.shape[0]
    own = sensors // GROUP
    sensor_index = lax.axis_index("sensor")
    slot_index = lax.axis_index("slot")
    day_index = lax.axis_index("day")
    z, y = sensor_index // NY, lax.rem(sensor_index, NY)
    core = lax.rem(slot_index, 2)
    x_hi = slot_index // 2
    x = x_hi * 2 + day_index

    def device(z, y, x, core):
        return (z * NY + y, (x // 2) * 2 + core, lax.rem(x, 2))

    def chunk_of(x, core):
        return ((x // 2) * 2 + core) * 2 + lax.rem(x, 2)

    def group_device(index):
        return (sensor_index, index // 2, lax.rem(index, 2))

    me = chunk_of(x, core)

    barrier = pltpu.get_barrier_semaphore()

    def greet(target):
        pl.semaphore_signal(barrier, inc=1, device_id=target, device_id_type=MESH)

    def greet_group(k, carry):
        greet(group_device(lax.rem(me + k, GROUP)))
        return carry

    def greet_z(k, carry):
        greet(device(lax.rem(z + k, NZ), y, x, core))
        return carry

    def greet_y(k, carry):
        other = lax.rem(y + k, NY)
        for cx, cc in ((0, 0), (0, 1), (2, 0), (2, 1), (None, 0)):
            if cx is None:
                greet(device(z, other, x_hi * 2 + 1 - day_index, core))
            else:
                greet(device(z, other, lax.rem(x + cx, NX), lax.rem(core + cc, 2)))
        return carry

    lax.fori_loop(1, GROUP, greet_group, 0)
    lax.fori_loop(1, NZ, greet_z, 0)
    lax.fori_loop(1, NY, greet_y, 0)

    loads = []
    for k in range(days):
        copy = pltpu.make_async_copy(traffic.at[k], t_all.at[pl.ds(k * slots, slots)], load_sem.at[k])
        copy.start()
        loads.append(copy)

    slot_local = slot_ref[pl.ds(pl.multiple_of(slot_index * slots, 8), slots), :]
    khatri = [slot_local * day_ref[pl.ds(day_index * days + k, 1), :] for k in range(days)]
    khatri = jnp.concatenate(khatri + [jnp.zeros((padded - rows, R), f32)], axis=0)
    w_high, w_low = split(khatri)
    w_cat[:, 0:R] = w_high
    w_cat[:, R:] = w_low
    t_all[pl.ds(rows, padded - rows), :] = jnp.zeros((padded - rows, sensors), f32)
    gathered[...] = jnp.zeros_like(gathered)
    c_wide[...] = jnp.zeros_like(c_wide)
    c_low[...] = jnp.zeros_like(c_low)
    for copy in loads:
        copy.wait()

    def convert(i, carry):
        lanes = pl.ds(pl.multiple_of(i * R, R), R)
        t_high[:, lanes], t_low[:, lanes] = split(t_all[:, lanes])
        return carry

    lax.fori_loop(0, sensors // R, convert, 0)

    def window_of(chunk):
        return pl.ds(pl.multiple_of(chunk * STRIDE, R), WINDOW)

    def rows_of(chunk):
        return pl.ds(pl.multiple_of(chunk * SHIFT, SHIFT), own)

    def first_product(chunk, target):
        lanes = window_of(chunk)
        wide = dot(t_high[:, lanes], w_cat[...], ((0,), (0,)))
        low = dot(t_low[:, lanes], w_cat[:, 0:R], ((0,), (0,)))
        target[...] = wide[:, 0:R] + wide[:, R:] + low

    def target_x(j):
        return lax.rem(x + jnp.where(j == 0, 2, jnp.where(j == 1, 1, jnp.where(j == 2, 3, 0))), NX)

    def sibling_copy(j):
        chunk = chunk_of(target_x(j), 1 - core)
        return pltpu.make_async_remote_copy(
            src_ref=win_sib.at[j].at[rows_of(chunk)], dst_ref=sib_recv.at[j],
            send_sem=sib_ssem.at[j], recv_sem=sib_rsem.at[j],
            device_id=device(z, y, x, 1 - core), device_id_type=MESH,
        )

    def x_copy(j):
        return pltpu.make_async_remote_copy(
            src_ref=x_send.at[j], dst_ref=x_recv.at[j],
            send_sem=x_ssem.at[j], recv_sem=x_rsem.at[j],
            device_id=device(z, y, target_x(j), core), device_id_type=MESH,
        )

    def scatter_step(j, carry):
        @pl.when(j < NX)
        def _():
            first_product(chunk_of(target_x(j), 1 - core), win_sib.at[j])

            @pl.when(j == 0)
            def _():
                pl.semaphore_wait(barrier, 7 + (NZ - 1) + 5 * (NY - 1))

            sibling_copy(j).start()
            first_product(chunk_of(target_x(j), core), win_own.at[j])

        @pl.when(j > 0)
        def _():
            sibling_copy(j - 1).wait_recv()
            x_send[j - 1] = win_own[j - 1, rows_of(chunk_of(target_x(j - 1), core)), :] + sib_recv[j - 1]

            @pl.when(j < NX)
            def _():
                x_copy(j - 1).start()

        return carry

    lax.fori_loop(0, NX + 1, scatter_step, 0)

    gram_day = gram_of(day_ref[...])
    inv_sensor = inverse(regularize(gram_of(slot_ref[...]) * gram_day))

    right_side = x_send[NX - 1]
    for j in range(NX - 1):
        x_copy(j).wait_recv()
        right_side = right_side + x_recv[j]
    sensor_raw = dot(right_side, inv_sensor, precision=highest)
    gathered[me, rows_of(me), :] = sensor_raw

    def device_y(p):
        return device(z, p, x, core)

    def device_z(p):
        return device(p, y, x, core)

    gram = gram_of(sensor_raw)
    for i in range(GROUP):
        gram_part[i] = gram[16 * i : 16 * i + 16]
    gx = Exchange((gx_buf, gx_s, gx_r), GROUP, me, group_device, gram_part)
    gy = Exchange((gy_buf, gy_s, gy_r), NY, y, device_y)
    gz = Exchange((gz_buf, gz_s, gz_r), NZ, z, device_z)
    ga = Exchange((ga_buf, ga_s, ga_r), GROUP, me, group_device)
    gx.start()
    gx_buf[me] = gram_part[me]

    def gather_copy(j, sender=False):
        chunk = me if sender else chunk_of(source_x(j), core)
        place = gathered.at[chunk].at[rows_of(chunk)]
        return pltpu.make_async_remote_copy(
            src_ref=place, dst_ref=place, send_sem=gat_ssem.at[j], recv_sem=gat_rsem.at[j],
            device_id=device(z, y, target_x(j), core), device_id_type=MESH,
        )

    def source_x(j):
        return lax.rem(x + jnp.where(j == 0, 2, jnp.where(j == 1, 3, jnp.where(j == 2, 1, 0))), NX)

    def forward_copy(j, sender=False):
        chunk = chunk_of(source_x(j), core if sender else 1 - core)
        place = gathered.at[chunk].at[rows_of(chunk)]
        return pltpu.make_async_remote_copy(
            src_ref=place, dst_ref=place, send_sem=fwd_ssem.at[j], recv_sem=fwd_rsem.at[j],
            device_id=device(z, y, x, 1 - core), device_id_type=MESH,
        )

    for j in (1, 2, 0):
        gather_copy(j, True).start()
    forward_copy(3, True).start()

    def second_product(chunk):
        lanes = window_of(chunk)
        high, low = split(gathered[chunk])
        c_wide[...] += dot(t_high[:, lanes], jnp.concatenate([high, low], axis=1))
        c_low[...] += dot(t_low[:, lanes], high)

    def gather_step(i, carry):
        j = 3 - i
        j = jnp.where(i == 0, 3, jnp.where(i == 1, 1, jnp.where(i == 2, 2, 0)))

        @pl.when(i > 0)
        def _():
            gather_copy(j).wait_recv()
            forward_copy(j, True).start()

        second_product(chunk_of(source_x(j), core))
        forward_copy(j).wait_recv()
        second_product(chunk_of(source_x(j), 1 - core))

        @pl.when(i == 1)
        def _():
            gx.wait_recv()
            gy_buf[y] = gx.total()
            gy.start()

        @pl.when(i == 2)
        def _():
            gy.wait_recv()
            gz_buf[z] = gy.total()
            gz.start()

        return carry

    lax.fori_loop(0, NX, gather_step, 0)

    contracted = c_wide[:, 0:R] + c_wide[:, R:] + c_low[...]
    contracted = [contracted[k * slots : (k + 1) * slots] for k in range(days)]
    part = contracted[0] * day_ref[pl.ds(day_index * days, 1), :]
    for k in range(1, days):
        part = part + contracted[k] * day_ref[pl.ds(day_index * days + k, 1), :]
    piece = slots // 8
    for i in range(8):
        slot_part[i, 0:piece] = part[i * piece : (i + 1) * piece]
        slot_part[i, piece:] = jnp.zeros((SLOT_PIECE - piece, R), f32)

    def device_8(p):
        return device(z, p // 2, x_hi * 2 + lax.rem(p, 2), core)

    def device_slot(p):
        return (sensor_index, p, day_index)

    me_8 = y * 2 + day_index
    s8 = Exchange((s8_buf, s8_s, s8_r), 8, me_8, device_8, slot_part)
    sz = Exchange((sz_buf, sz_s, sz_r), NZ, z, device_z)
    sa = Exchange((sa_buf, sa_s, sa_r), 8, me_8, device_8)
    sx = Exchange((sx_buf, sx_s, sx_r), 4, slot_index, device_slot)
    s8.start()
    s8_buf[me_8] = slot_part[me_8]
    s8.wait_recv()
    sz_buf[z] = s8.total()
    sz.start()

    gz.wait_recv()
    ga_buf[me] = gz.total()
    ga.start()
    ga.wait_recv()
    gram = jnp.concatenate([ga_buf[i] for i in range(GROUP)], axis=0)

    def norms_of(gram, count):
        square = jnp.where(diagonal_mask(), gram, 0.0)
        row = jnp.sqrt(jnp.sum(square, axis=0, keepdims=True) / count + epsilon)
        column = jnp.sqrt(jnp.sum(square, axis=1, keepdims=True) / count + epsilon)
        return row, gram / (column * row)

    sensor_norms, gram_sensor = norms_of(gram, sensor_count)
    sensor_out[...] = gathered[me, rows_of(me), :] / sensor_norms
    inv_slot = inverse(regularize(gram_sensor * gram_day))

    sz.wait_recv()
    sa_buf[me_8] = sz.total()
    sa.start()
    sa.wait_recv()
    slot_rhs = jnp.concatenate([sa_buf[i][0:piece] for i in range(8)], axis=0) / sensor_norms
    slot_raw = dot(slot_rhs, inv_slot, precision=highest)
    sx_buf[slot_index] = slot_raw
    sx.start()
    sx.wait_recv()
    gram = gram_of(sx_buf[0])
    for i in range(1, 4):
        gram = gram + gram_of(sx_buf[i])
    slot_norms, gram_slot_new = norms_of(gram, slot_count)
    slot_new = slot_raw / slot_norms
    slot_out[...] = slot_new

    weight = slot_new / sensor_norms
    day_part = [jnp.sum(c * weight, axis=0, keepdims=True) for c in contracted]
    day_part = jnp.concatenate(day_part + [jnp.zeros((8 - days, R), f32)], axis=0)

    def device_16(p):
        return (z * NY + p // 4, lax.rem(p, 4), day_index)

    me_16 = y * 4 + slot_index
    dy = Exchange((dy_buf, dy_s, dy_r), 16, me_16, device_16)
    dz = Exchange((dz_buf, dz_s, dz_r), NZ, z, device_z)
    dy_buf[me_16] = day_part
    dy.start()
    inv_day = inverse(regularize(gram_sensor * gram_slot_new))
    dy.wait_recv()
    dz_buf[z] = dy.total()
    dz.start()
    dz.wait_recv()
    day_new = dot(dz.total(), inv_day, precision=highest)
    day_out[...] = day_new[0:days]

    def drain(j, carry):
        sibling_copy(j).wait_send()
        forward_copy(j, True).wait_send()

        @pl.when(j < NX - 1)
        def _():
            x_copy(j).wait_send()
            gather_copy(j, True).wait_send()

        return carry

    lax.fori_loop(0, NX, drain, 0)
    for exchange in (gx, gy, gz, ga, s8, sz, sa, sx, dy, dz):
        exchange.wait_send()


def on_device(traffic, slot_factor, day_factor):
    days, slots, sensors = traffic.shape
    slot_count = slot_factor.shape[0]
    sensor_count = sensors * lax.axis_size("sensor")
    own = sensors // GROUP
    padded = (days * slots + 15) // 16 * 16

    def exchange_scratch(count, *block):
        return [
            pltpu.VMEM((count, *block), f32),
            pltpu.SemaphoreType.DMA((count,)),
            pltpu.SemaphoreType.DMA((count,)),
        ]

    dma = pltpu.SemaphoreType.DMA
    scratch = [
        pltpu.VMEM((padded, sensors), f32),
        pltpu.VMEM((padded, sensors), bf16),
        pltpu.VMEM((padded, sensors), bf16),
        pltpu.VMEM((padded, 2 * R), bf16),
        dma((days,)),
        pltpu.VMEM((NX, WINDOW, R), f32),
        pltpu.VMEM((NX, WINDOW, R), f32),
        *exchange_scratch(NX, own, R),
        pltpu.VMEM((NX, own, R), f32),
        *exchange_scratch(NX - 1, own, R),
        pltpu.VMEM((GROUP, WINDOW, R), f32),
        dma((NX - 1,)), dma((NX - 1,)), dma((NX,)), dma((NX,)),
        pltpu.VMEM((padded, 2 * R), f32),
        pltpu.VMEM((padded, R), f32),
        pltpu.VMEM((GROUP, 16, R), f32),
        *exchange_scratch(GROUP, 16, R),
        *exchange_scratch(NY, 16, R),
        *exchange_scratch(NZ, 16, R),
        *exchange_scratch(GROUP, 16, R),
        pltpu.VMEM((8, SLOT_PIECE, R), f32),
        *exchange_scratch(8, SLOT_PIECE, R),
        *exchange_scratch(NZ, SLOT_PIECE, R),
        *exchange_scratch(8, SLOT_PIECE, R),
        *exchange_scratch(4, slots, R),
        *exchange_scratch(16, 8, R),
        *exchange_scratch(NZ, 8, R),
    ]
    vmem = pl.BlockSpec(memory_space=pltpu.VMEM)

    def kernel(*refs):
        body(sensor_count, slot_count, *refs)

    return pl.pallas_call(
        kernel,
        out_shape=(
            jax.ShapeDtypeStruct((own, R), f32),
            jax.ShapeDtypeStruct((slots, R), f32),
            jax.ShapeDtypeStruct((days, R), f32),
        ),
        in_specs=[pl.BlockSpec(memory_space=pl.ANY), vmem, vmem],
        out_specs=(vmem, vmem, vmem),
        scratch_shapes=scratch,
        compiler_params=pltpu.CompilerParams(
            collective_id=0, has_side_effects=True, vmem_limit_bytes=48 * 1024 * 1024
        ),
    )(traffic, slot_factor, day_factor)


def solution(mesh):
    in_specs = (P("day", "slot", "sensor"), P(), P())
    out_specs = (P(("sensor", "slot", "day"), None), P("slot", None), P("day", None))
    return jax.shard_map(
        on_device, mesh=mesh, in_specs=in_specs, out_specs=out_specs, check_vma=False
    )
```

```python
import jax
import jax.numpy as jnp
from jax import lax
from jax.experimental import pallas as pl
from jax.experimental.pallas import tpu as pltpu
from jax.sharding import PartitionSpec as P

MESH = pl.DeviceIdType.MESH
highest = lax.Precision.HIGHEST
f32 = jnp.float32
bf16 = jnp.bfloat16
ridge_scale = 0.001
epsilon = 1e-05

R = 128
NX, NY, NZ = 4, 4, 16
GROUP = 8
WINDOW, STRIDE, SHIFT = 512, 384, 16


def dot(a, b, contract=((1,), (0,)), precision=None):
    return lax.dot_general(a, b, (contract, ((), ())), precision=precision, preferred_element_type=f32)


def gram_of(rows):
    return dot(rows, rows, ((0,), (0,)), highest)


def diagonal_mask():
    return lax.broadcasted_iota(jnp.int32, (R, R), 0) == lax.broadcasted_iota(jnp.int32, (R, R), 1)


def regularize(matrix):
    eye = diagonal_mask()
    mean = jnp.sum(jnp.where(eye, matrix, 0.0)) / R
    return matrix + jnp.where(eye, ridge_scale * mean, 0.0)


def inverse(matrix):
    lane = lax.broadcasted_iota(jnp.int32, (8, R), 1)
    sub = lax.broadcasted_iota(jnp.int32, (8, R), 0)
    lane_rest = lax.broadcasted_iota(jnp.int32, (R - 8, R), 1)

    def step(_, matrix):
        top, rest = matrix[0:8], matrix[8:]
        rows = [jnp.broadcast_to(top[i : i + 1, :], (8, R)) for i in range(8)]
        a = {(i, j): jnp.broadcast_to(rows[i][:, j : j + 1], (8, R)) for i in range(8) for j in range(i, 8)}
        rows = [jnp.where(lane == i, 1.0, jnp.where(lane < 8, 0.0, rows[i])) for i in range(8)]
        lower, scale = {}, []
        for t in range(8):
            scale.append(1.0 / a[t, t])
            for s in range(t + 1, 8):
                lower[s, t] = a[t, s] * scale[t]
            for s in range(t + 1, 8):
                for u in range(s, 8):
                    a[s, u] = a[s, u] - lower[s, t] * a[t, u]
                rows[s] = rows[s] - lower[s, t] * rows[t]
        rows = [rows[t] * scale[t] for t in range(8)]
        for t in range(7, -1, -1):
            for s in range(t):
                rows[s] = rows[s] - lower[t, s] * rows[t]
        new_top = rows[7]
        for i in range(7):
            new_top = jnp.where(sub == i, rows[i], new_top)
        base = jnp.where(lane_rest < 8, 0.0, rest)
        for i in range(8):
            base = base - rest[:, i : i + 1] * rows[i][0:1, :]
        return pltpu.roll(jnp.concatenate([base, new_top], axis=0), R - 8, 1)

    return lax.fori_loop(0, R // 8, step, matrix)


def split(value):
    high = value.astype(bf16)
    return high, (value - high.astype(f32)).astype(bf16)


class Exchange:
    def __init__(self, refs, count, me, device, source=None):
        self.buffer, self.send_sem, self.recv_sem = refs
        self.count, self.me, self.device, self.source = count, me, device, source

    def copy(self, k, slot):
        peer = lax.rem(self.me + k, self.count)
        source = self.buffer.at[self.me] if self.source is None else self.source.at[peer]
        return pltpu.make_async_remote_copy(
            src_ref=source,
            dst_ref=self.buffer.at[self.me if slot is None else peer],
            send_sem=self.send_sem.at[k],
            recv_sem=self.recv_sem.at[self.me if slot is None else peer],
            device_id=self.device(peer),
            device_id_type=MESH,
        )

    def each(self, act):
        middle = self.count // 2

        def step(i, carry):
            act(middle + jnp.where(lax.rem(i, 2) == 1, (i + 1) // 2, -(i // 2)))
            return carry

        lax.fori_loop(0, self.count - 1, step, 0)

    def start(self):
        self.each(lambda k: self.copy(k, None).start())

    def wait_recv(self):
        self.each(lambda k: self.copy(k, "peer").wait_recv())

    def wait_send(self):
        self.each(lambda k: self.copy(k, None).wait_send())

    def total(self):
        total = self.buffer[0]
        for i in range(1, self.count):
            total = total + self.buffer[i]
        return total


def body(
    sensor_count, slot_count,
    traffic, slot_in, day_in, sensor_out, slot_out, day_out,
    slot_ref, day_ref, t_win, t_high, t_low, w_cat, factor_sem, load_sem,
    win_sib, win_own, sib_recv, sib_ssem, sib_rsem, x_send, x_recv, x_ssem, x_rsem,
    gathered, gat_ssem, gat_rsem, fwd_ssem, fwd_rsem,
    c_wide, c_low,
    gram_part, gram_rows, gx_buf, gx_s, gx_r, gy_buf, gy_s, gy_r, gz_buf, gz_s, gz_r, ga_buf, ga_s, ga_r,
    slot_part, s8_buf, s8_s, s8_r, sz_buf, sz_s, sz_r, sa_buf, sa_s, sa_r, slot_all,
    con_part, con_rows, cy_buf, cy_s, cy_r, cz_buf, cz_s, cz_r, ca_buf, ca_s, ca_r, weights,
    dy_buf, dy_s, dy_r,
):
    days, slots, sensors = traffic.shape
    rows = days * slots
    padded = w_cat.shape[0]
    strips = NZ // days
    strip = slots // NY // strips
    own = sensors // GROUP
    sensor_index = lax.axis_index("sensor")
    slot_index = lax.axis_index("slot")
    day_index = lax.axis_index("day")
    z, y = sensor_index // NY, lax.rem(sensor_index, NY)
    core = lax.rem(slot_index, 2)
    x_hi = slot_index // 2
    x = x_hi * 2 + day_index

    def device(z, y, x, core):
        return (z * NY + y, (x // 2) * 2 + core, lax.rem(x, 2))

    def chunk_of(x, core):
        return ((x // 2) * 2 + core) * 2 + lax.rem(x, 2)

    def group_device(index):
        return (sensor_index, index // 2, lax.rem(index, 2))

    me = chunk_of(x, core)

    barrier = pltpu.get_barrier_semaphore()

    def greet(target):
        pl.semaphore_signal(barrier, inc=1, device_id=target, device_id_type=MESH)

    def greet_group(k, carry):
        greet(group_device(lax.rem(me + k, GROUP)))
        return carry

    def greet_z(k, carry):
        greet(device(lax.rem(z + k, NZ), y, x, core))
        return carry

    def greet_y(k, carry):
        other = lax.rem(y + k, NY)
        for cx, cc in ((0, 0), (0, 1), (2, 0), (2, 1), (None, 0)):
            if cx is None:
                greet(device(z, other, x_hi * 2 + 1 - day_index, core))
            else:
                greet(device(z, other, lax.rem(x + cx, NX), lax.rem(core + cc, 2)))
        return carry

    lax.fori_loop(1, GROUP, greet_group, 0)
    lax.fori_loop(1, NZ, greet_z, 0)
    lax.fori_loop(1, NY, greet_y, 0)

    factor_loads = [
        pltpu.make_async_copy(slot_in, slot_ref, factor_sem.at[0]),
        pltpu.make_async_copy(day_in, day_ref, factor_sem.at[1]),
    ]
    for copy in factor_loads:
        copy.start()

    def target_x(j):
        return lax.rem(x + jnp.where(j == 0, 2, jnp.where(j == 1, 1, jnp.where(j == 2, 3, 0))), NX)

    def load_copy(chunk):
        lanes = pl.ds(pl.multiple_of(chunk * STRIDE, R), WINDOW)
        return pltpu.make_async_copy(traffic.at[:, :, lanes], t_win.at[chunk], load_sem.at[chunk])

    def load_step(j, carry):
        load_copy(chunk_of(target_x(j), 1 - core)).start()
        load_copy(chunk_of(target_x(j), core)).start()
        return carry

    lax.fori_loop(0, NX, load_step, 0)

    for c in range(GROUP):
        if c:
            gathered[c, 0 : SHIFT * c] = jnp.zeros((SHIFT * c, R), f32)
        if SHIFT * c + own < WINDOW:
            gathered[c, SHIFT * c + own :] = jnp.zeros((WINDOW - own - SHIFT * c, R), f32)
    c_wide[...] = jnp.zeros_like(c_wide)
    c_low[...] = jnp.zeros_like(c_low)
    for copy in factor_loads:
        copy.wait()

    slot_local = slot_ref[pl.ds(pl.multiple_of(slot_index * slots, 8), slots), :]
    khatri = [slot_local * day_ref[pl.ds(day_index * days + k, 1), :] for k in range(days)]
    khatri = jnp.concatenate(khatri + [jnp.zeros((padded - rows, R), f32)], axis=0)
    w_high, w_low = split(khatri)
    w_cat[:, 0:R] = w_high
    w_cat[:, R:] = w_low

    half = own // 2

    def rows_of(chunk):
        return pl.ds(pl.multiple_of(chunk * SHIFT, SHIFT), own)

    def half_rows_of(chunk, h):
        return pl.ds(pl.multiple_of(chunk * SHIFT + h * half, 8), half)

    def first_product(chunk, target):
        load_copy(chunk).wait()
        block = [t_win[chunk, k] for k in range(days)] + [jnp.zeros((padded - rows, WINDOW), f32)]
        high, low = split(jnp.concatenate(block, axis=0))
        t_high[chunk] = high
        t_low[chunk] = low
        wide = dot(high, w_cat[...], ((0,), (0,)))
        target[...] = wide[:, 0:R] + wide[:, R:] + dot(low, w_cat[:, 0:R], ((0,), (0,)))

    def sibling_copy(j):
        chunk = chunk_of(target_x(j), 1 - core)
        return pltpu.make_async_remote_copy(
            src_ref=win_sib.at[j].at[rows_of(chunk)], dst_ref=sib_recv.at[j],
            send_sem=sib_ssem.at[j], recv_sem=sib_rsem.at[j],
            device_id=device(z, y, x, 1 - core), device_id_type=MESH,
        )

    def x_copy(j, h):
        rows_h = pl.ds(pl.multiple_of(h * half, 8), half)
        return pltpu.make_async_remote_copy(
            src_ref=x_send.at[j].at[rows_h], dst_ref=x_recv.at[j].at[rows_h],
            send_sem=x_ssem.at[j, h], recv_sem=x_rsem.at[j, h],
            device_id=device(z, y, target_x(j), core), device_id_type=MESH,
        )

    def scatter_step(j, carry):
        @pl.when(j < NX)
        def _():
            first_product(chunk_of(target_x(j), 1 - core), win_sib.at[j])
            first_product(chunk_of(target_x(j), core), win_own.at[j])

            @pl.when(j == 0)
            def _():
                pl.semaphore_wait(barrier, 7 + (NZ - 1) + 5 * (NY - 1))

            sibling_copy(j).start()

        @pl.when(j > 0)
        def _():
            sibling_copy(j - 1).wait_recv()
            x_send[j - 1] = win_own[j - 1, rows_of(chunk_of(target_x(j - 1), core)), :] + sib_recv[j - 1]

            @pl.when(j < NX)
            def _():
                x_copy(j - 1, 0).start()

        return carry

    lax.fori_loop(0, NX + 1, scatter_step, 0)
    for j in range(NX - 1):
        x_copy(j, 1).start()

    gram_day = gram_of(day_ref[...])
    inv_sensor = inverse(regularize(gram_of(slot_ref[...]) * gram_day))

    def own_half(h):
        total = x_send[NX - 1, h * half : (h + 1) * half]
        for j in range(NX - 1):
            x_copy(j, h).wait_recv()
            total = total + x_recv[j, h * half : (h + 1) * half]
        sensor_raw = dot(total, inv_sensor, precision=highest)
        gathered[me, half_rows_of(me, h), :] = sensor_raw
        return gram_of(sensor_raw)

    def device_y(p):
        return device(z, p, x, core)

    def device_z(p):
        return device(p, y, x, core)

    def device_32(p):
        return (z * NY + p // 8, lax.rem(p // 2, 4), lax.rem(p, 2))

    me_32 = y * 8 + me
    gx = Exchange((gx_buf, gx_s, gx_r), GROUP, me, group_device, gram_part)
    gy = Exchange((gy_buf, gy_s, gy_r), NY, y, device_y, gram_rows)
    gz = Exchange((gz_buf, gz_s, gz_r), NZ, z, device_z)
    ga = Exchange((ga_buf, ga_s, ga_r), 32, me_32, device_32)

    def source_x(j):
        return lax.rem(x + jnp.where(j == 0, 2, jnp.where(j == 1, 3, jnp.where(j == 2, 1, 0))), NX)

    def gather_copy(j, h, sender=False):
        chunk = me if sender else chunk_of(source_x(j), core)
        place = gathered.at[chunk].at[half_rows_of(chunk, h)]
        return pltpu.make_async_remote_copy(
            src_ref=place, dst_ref=place, send_sem=gat_ssem.at[j, h], recv_sem=gat_rsem.at[j, h],
            device_id=device(z, y, target_x(j), core), device_id_type=MESH,
        )

    def forward_copy(j, h, sender=False):
        chunk = chunk_of(source_x(j), core if sender else 1 - core)
        place = gathered.at[chunk].at[half_rows_of(chunk, h)]
        return pltpu.make_async_remote_copy(
            src_ref=place, dst_ref=place, send_sem=fwd_ssem.at[j, h], recv_sem=fwd_rsem.at[j, h],
            device_id=device(z, y, x, 1 - core), device_id_type=MESH,
        )

    def gather_start(h):
        for j in (1, 2, 0):
            gather_copy(j, h, True).start()
        forward_copy(3, h, True).start()

    gram = own_half(0)
    gather_start(0)
    gram = gram + own_half(1)
    for i in range(GROUP):
        gram_part[i] = gram[16 * i : 16 * i + 16]
    gx.start()
    gx_buf[me] = gram_part[me]
    gather_start(1)

    def second_product(chunk):
        high, low = split(gathered[chunk])
        c_wide[...] += dot(t_high[chunk], jnp.concatenate([high, low], axis=1))
        c_low[...] += dot(t_low[chunk], high)

    def own_core(j):
        second_product(chunk_of(source_x(j), core))

    def other_core(j):
        forward_copy(j, 0).wait_recv()
        forward_copy(j, 1).wait_recv()
        second_product(chunk_of(source_x(j), 1 - core))

    def pass_on(j, h):
        gather_copy(j, h).wait_recv()
        forward_copy(j, h, True).start()

    def gather_step(i, carry):
        @pl.when(i == 0)
        def _():
            own_core(3)
            other_core(3)
            pass_on(1, 0)
            pass_on(2, 0)
            pass_on(0, 0)
            gx.wait_recv()
            gram = gx.total()
            for i in range(NY):
                gram_rows[i] = gram[4 * i : 4 * i + 4]
            gy.start()
            gy_buf[y] = gram_rows[y]
            pass_on(1, 1)
            pass_on(2, 1)

        @pl.when(i == 3)
        def _():
            pass_on(0, 1)

        j = jnp.where(i == 0, 1, jnp.where(i == 1, 2, 0))

        @pl.when(i != 2)
        def _():
            own_core(j)

        @pl.when(i == 2)
        def _():
            gy.wait_recv()
            gz_buf[z] = gy.total()
            gz.start()

        @pl.when(i >= 2)
        def _():
            other_core(jnp.where(i == 2, 1, 0))

        @pl.when(i == 2)
        def _():
            other_core(2)

        return carry

    lax.fori_loop(0, NX, gather_step, 0)

    contracted = c_wide[:, 0:R] + c_wide[:, R:] + c_low[...]
    contracted = [contracted[k * slots : (k + 1) * slots] for k in range(days)]
    part = contracted[0] * day_ref[pl.ds(day_index * days, 1), :]
    for k in range(1, days):
        part = part + contracted[k] * day_ref[pl.ds(day_index * days + k, 1), :]
    piece = slots // 8
    for i in range(8):
        slot_part[i] = part[i * piece : (i + 1) * piece]

    def device_8(p):
        return device(z, p // 2, x_hi * 2 + lax.rem(p, 2), core)

    me_8 = y * 2 + day_index
    s8 = Exchange((s8_buf, s8_s, s8_r), 8, me_8, device_8, slot_part)
    sz = Exchange((sz_buf, sz_s, sz_r), NZ, z, device_z)
    sa = Exchange((sa_buf, sa_s, sa_r), 32, me_32, device_32)
    s8.start()
    s8_buf[me_8] = slot_part[me_8]

    for p in range(NY):
        for k in range(days):
            for m in range(strips):
                row = (p * strips + m) * strip
                con_part[p, k * strips + m] = contracted[k][row : row + strip]
        for i in range(days * strips, NZ):
            con_part[p, i] = jnp.zeros((strip, R), f32)
    cy = Exchange((cy_buf, cy_s, cy_r), NY, y, device_y, con_part)
    cz = Exchange((cz_buf, cz_s, cz_r), NZ, z, device_z, con_rows)
    ca = Exchange((ca_buf, ca_s, ca_r), NZ, z, device_z)
    cy.start()
    cy_buf[y] = con_part[y]

    s8.wait_recv()
    sz_buf[z] = s8.total()
    sz.start()

    cy.wait_recv()
    con_rows[...] = cy.total()
    cz.start()
    cz_buf[z] = con_rows[z]

    gz.wait_recv()
    ga_buf[me_32] = gz.total()
    ga.start()
    sz.wait_recv()
    sa_buf[me_32] = sz.total()
    sa.start()
    cz.wait_recv()
    ca_buf[z] = cz.total()
    ca.start()
    ga.wait_recv()
    gram = jnp.concatenate([ga_buf[i * GROUP + g] for g in range(GROUP) for i in range(NY)], axis=0)

    def norms_of(gram, count):
        square = jnp.where(diagonal_mask(), gram, 0.0)
        row = jnp.sqrt(jnp.sum(square, axis=0, keepdims=True) / count + epsilon)
        column = jnp.sqrt(jnp.sum(square, axis=1, keepdims=True) / count + epsilon)
        return row, gram / (column * row)

    sensor_norms, gram_sensor = norms_of(gram, sensor_count)
    sensor_out[...] = gathered[me, rows_of(me), :] / sensor_norms
    inv_slot = inverse(regularize(gram_sensor * gram_day))

    sa.wait_recv()
    slot_rhs = [sa_buf[(i // 2) * 8 + s * 2 + i % 2] for s in range(4) for i in range(8)]
    slot_rhs = jnp.concatenate(slot_rhs, axis=0) / sensor_norms
    slot_all[...] = dot(slot_rhs, inv_slot, precision=highest)
    gram = gram_of(slot_all[...])
    slot_norms, gram_slot_new = norms_of(gram, slot_count)
    slot_new = slot_all[pl.ds(pl.multiple_of(slot_index * slots, 8), slots), :] / slot_norms
    slot_out[...] = slot_new

    weight = slot_new / sensor_norms
    for i in range(NY * strips):
        weights[i] = weight[i * strip : (i + 1) * strip]
    ca.wait_recv()
    for k in range(days):
        total = ca_buf[k * strips] * weights[y * strips]
        for m in range(1, strips):
            total = total + ca_buf[k * strips + m] * weights[y * strips + m]
        dy_buf[y * 4 + slot_index, k : k + 1] = jnp.sum(total, axis=0, keepdims=True)

    def device_16(p):
        return (z * NY + p // 4, lax.rem(p, 4), day_index)

    me_16 = y * 4 + slot_index
    dy = Exchange((dy_buf, dy_s, dy_r), 16, me_16, device_16)
    dy.start()
    inv_day = inverse(regularize(gram_sensor * gram_slot_new))
    dy.wait_recv()
    day_out[...] = dot(dy.total(), inv_day, precision=highest)

    def drain(j, carry):
        sibling_copy(j).wait_send()
        for h in range(2):
            forward_copy(j, h, True).wait_send()

        @pl.when(j < NX - 1)
        def _():
            for h in range(2):
                x_copy(j, h).wait_send()
                gather_copy(j, h, True).wait_send()

        return carry

    lax.fori_loop(0, NX, drain, 0)
    for exchange in (gx, gy, gz, ga, s8, sz, sa, cy, cz, ca, dy):
        exchange.wait_send()


def on_device(traffic, slot_factor, day_factor):
    days, slots, sensors = traffic.shape
    slot_count = slot_factor.shape[0]
    sensor_count = sensors * lax.axis_size("sensor")
    own = sensors // GROUP
    padded = (days * slots + 15) // 16 * 16
    strip = slots // NY // (NZ // days)

    def exchange_scratch(count, *block):
        return [
            pltpu.VMEM((count, *block), f32),
            pltpu.SemaphoreType.DMA((count,)),
            pltpu.SemaphoreType.DMA((count,)),
        ]

    dma = pltpu.SemaphoreType.DMA
    scratch = [
        pltpu.VMEM(slot_factor.shape, f32),
        pltpu.VMEM(day_factor.shape, f32),
        pltpu.VMEM((GROUP, days, slots, WINDOW), f32),
        pltpu.VMEM((GROUP, padded, WINDOW), bf16),
        pltpu.VMEM((GROUP, padded, WINDOW), bf16),
        pltpu.VMEM((padded, 2 * R), bf16),
        dma((2,)),
        dma((GROUP,)),
        pltpu.VMEM((NX, WINDOW, R), f32),
        pltpu.VMEM((NX, WINDOW, R), f32),
        *exchange_scratch(NX, own, R),
        pltpu.VMEM((NX, own, R), f32),
        pltpu.VMEM((NX - 1, own, R), f32),
        dma((NX - 1, 2)), dma((NX - 1, 2)),
        pltpu.VMEM((GROUP, WINDOW, R), f32),
        dma((NX - 1, 2)), dma((NX - 1, 2)), dma((NX, 2)), dma((NX, 2)),
        pltpu.VMEM((padded, 2 * R), f32),
        pltpu.VMEM((padded, R), f32),
        pltpu.VMEM((GROUP, 16, R), f32),
        pltpu.VMEM((NY, 4, R), f32),
        *exchange_scratch(GROUP, 16, R),
        *exchange_scratch(NY, 4, R),
        *exchange_scratch(NZ, 4, R),
        *exchange_scratch(32, 4, R),
        pltpu.VMEM((8, slots // 8, R), f32),
        *exchange_scratch(8, slots // 8, R),
        *exchange_scratch(NZ, slots // 8, R),
        *exchange_scratch(32, slots // 8, R),
        pltpu.VMEM(slot_factor.shape, f32),
        pltpu.VMEM((NY, NZ, strip, R), f32),
        pltpu.VMEM((NZ, strip, R), f32),
        *exchange_scratch(NY, NZ, strip, R),
        *exchange_scratch(NZ, strip, R),
        *exchange_scratch(NZ, strip, R),
        pltpu.VMEM((slots // strip, strip, R), f32),
        *exchange_scratch(16, days, R),
    ]
    vmem = pl.BlockSpec(memory_space=pltpu.VMEM)

    def kernel(*refs):
        body(sensor_count, slot_count, *refs)

    results = pl.pallas_call(
        kernel,
        out_shape=(
            jax.ShapeDtypeStruct((own, R), f32),
            jax.ShapeDtypeStruct((slots, R), f32),
            jax.ShapeDtypeStruct((days, R), f32),
        ),
        in_specs=[pl.BlockSpec(memory_space=pltpu.HBM)] * 3,
        out_specs=(vmem, vmem, vmem),
        scratch_shapes=scratch,
        compiler_params=pltpu.CompilerParams(
            collective_id=0, has_side_effects=True, vmem_limit_bytes=60 * 1024 * 1024
        ),
    )(traffic, slot_factor, day_factor)

    def store(*refs):
        for i in range(3):
            refs[3 + i][...] = refs[i][...]

    return pl.pallas_call(
        store,
        out_shape=tuple(jax.ShapeDtypeStruct(a.shape, f32) for a in results),
        in_specs=[vmem] * 3,
        out_specs=(vmem,) * 3,
    )(*results)


def solution(mesh):
    in_specs = (P("day", "slot", "sensor"), P(), P())
    out_specs = (P(("sensor", "slot", "day"), None), P("slot", None), P("day", None))
    return jax.shard_map(
        on_device, mesh=mesh, in_specs=in_specs, out_specs=out_specs, check_vma=False
    )
```

```python
import jax
import jax.numpy as jnp
from jax import lax
from jax.experimental import pallas as pl
from jax.experimental.pallas import tpu as pltpu
from jax.sharding import PartitionSpec as P

MESH = pl.DeviceIdType.MESH
highest = lax.Precision.HIGHEST
f32 = jnp.float32
bf16 = jnp.bfloat16
ridge_scale = 0.001
epsilon = 1e-05

R = 128
NX, NY, NZ = 4, 4, 16
GROUP = 8
WINDOW, STRIDE, SHIFT = 512, 384, 16


def dot(a, b, contract=((1,), (0,)), precision=None):
    return lax.dot_general(a, b, (contract, ((), ())), precision=precision, preferred_element_type=f32)


def gram_of(rows):
    return dot(rows, rows, ((0,), (0,)), highest)


def diagonal_mask():
    return lax.broadcasted_iota(jnp.int32, (R, R), 0) == lax.broadcasted_iota(jnp.int32, (R, R), 1)


def regularize(matrix):
    eye = diagonal_mask()
    mean = jnp.sum(jnp.where(eye, matrix, 0.0)) / R
    return matrix + jnp.where(eye, ridge_scale * mean, 0.0)


def inverse(matrix):
    lane = lax.broadcasted_iota(jnp.int32, (8, R), 1)
    sub = lax.broadcasted_iota(jnp.int32, (8, R), 0)
    lane_rest = lax.broadcasted_iota(jnp.int32, (R - 8, R), 1)

    def step(_, matrix):
        top, rest = matrix[0:8], matrix[8:]
        rows = [jnp.broadcast_to(top[i : i + 1, :], (8, R)) for i in range(8)]
        a = {(i, j): jnp.broadcast_to(rows[i][:, j : j + 1], (8, R)) for i in range(8) for j in range(i, 8)}
        rows = [jnp.where(lane == i, 1.0, jnp.where(lane < 8, 0.0, rows[i])) for i in range(8)]
        lower, scale = {}, []
        for t in range(8):
            scale.append(1.0 / a[t, t])
            for s in range(t + 1, 8):
                lower[s, t] = a[t, s] * scale[t]
            for s in range(t + 1, 8):
                for u in range(s, 8):
                    a[s, u] = a[s, u] - lower[s, t] * a[t, u]
                rows[s] = rows[s] - lower[s, t] * rows[t]
        rows = [rows[t] * scale[t] for t in range(8)]
        for t in range(7, -1, -1):
            for s in range(t):
                rows[s] = rows[s] - lower[t, s] * rows[t]
        new_top = rows[7]
        for i in range(7):
            new_top = jnp.where(sub == i, rows[i], new_top)
        base = jnp.where(lane_rest < 8, 0.0, rest)
        for i in range(8):
            base = base - rest[:, i : i + 1] * rows[i][0:1, :]
        return pltpu.roll(jnp.concatenate([base, new_top], axis=0), R - 8, 1)

    return lax.fori_loop(0, R // 8, step, matrix)


def split(value):
    high = value.astype(bf16)
    return high, (value - high.astype(f32)).astype(bf16)


class Exchange:
    def __init__(self, refs, count, me, device, source=None):
        self.buffer, self.send_sem, self.recv_sem = refs
        self.count, self.me, self.device, self.source = count, me, device, source

    def copy(self, k, slot):
        peer = lax.rem(self.me + k, self.count)
        source = self.buffer.at[self.me] if self.source is None else self.source.at[peer]
        return pltpu.make_async_remote_copy(
            src_ref=source,
            dst_ref=self.buffer.at[self.me if slot is None else peer],
            send_sem=self.send_sem.at[k],
            recv_sem=self.recv_sem.at[self.me if slot is None else peer],
            device_id=self.device(peer),
            device_id_type=MESH,
        )

    def each(self, act):
        middle = self.count // 2

        def step(i, carry):
            act(middle + jnp.where(lax.rem(i, 2) == 1, (i + 1) // 2, -(i // 2)))
            return carry

        lax.fori_loop(0, self.count - 1, step, 0)

    def start(self):
        self.each(lambda k: self.copy(k, None).start())

    def wait_recv(self):
        self.each(lambda k: self.copy(k, "peer").wait_recv())

    def wait_send(self):
        self.each(lambda k: self.copy(k, None).wait_send())

    def total(self):
        total = self.buffer[0]
        for i in range(1, self.count):
            total = total + self.buffer[i]
        return total


def body(
    sensor_count, slot_count,
    traffic, slot_in, day_in, sensor_out, slot_out, day_out,
    slot_ref, day_ref, t_win, t_high, t_low, w_cat, factor_sem, load_sem, round_sem,
    win_sib, win_own, sib_recv, sib_ssem, sib_rsem, x_send, x_recv, x_ssem, x_rsem,
    gathered, gat_ssem, gat_rsem, fwd_ssem, fwd_rsem,
    c_wide, c_low,
    gram_part, gram_rows, gx_buf, gx_s, gx_r, gy_buf, gy_s, gy_r, gz_buf, gz_s, gz_r, ga_buf, ga_s, ga_r,
    slot_part, s8_buf, s8_s, s8_r, sz_buf, sz_s, sz_r, sa_buf, sa_s, sa_r, slot_all,
    con_part, con_rows, cy_buf, cy_s, cy_r, cz_buf, cz_s, cz_r, ca_buf, ca_s, ca_r, weights,
    dy_buf, dy_s, dy_r,
):
    days, slots, sensors = traffic.shape
    rows = days * slots
    padded = w_cat.shape[0]
    strips = NZ // days
    strip = slots // NY // strips
    own = sensors // GROUP
    sensor_index = lax.axis_index("sensor")
    slot_index = lax.axis_index("slot")
    day_index = lax.axis_index("day")
    z, y = sensor_index // NY, lax.rem(sensor_index, NY)
    core = lax.rem(slot_index, 2)
    x_hi = slot_index // 2
    x = x_hi * 2 + day_index

    def device(z, y, x, core):
        return (z * NY + y, (x // 2) * 2 + core, lax.rem(x, 2))

    def chunk_of(x, core):
        return ((x // 2) * 2 + core) * 2 + lax.rem(x, 2)

    def group_device(index):
        return (sensor_index, index // 2, lax.rem(index, 2))

    me = chunk_of(x, core)

    barrier = pltpu.get_barrier_semaphore()

    def greet(target):
        pl.semaphore_signal(barrier, inc=1, device_id=target, device_id_type=MESH)

    def greet_group(k, carry):
        greet(group_device(lax.rem(me + k, GROUP)))
        return carry

    lax.fori_loop(1, GROUP, greet_group, 0)
    for k in range(1, NY):
        greet(device(z, lax.rem(y + k, NY), x, core))
    for k in (1, NZ - 1):
        greet(device(lax.rem(z + k, NZ), y, x, core))
    barrier_count = (GROUP - 1) + (NY - 1) + 2

    def round_z(i):
        for k in (2**i, NZ - 2**i):
            target = device(lax.rem(z + k, NZ), y, x, core)
            pl.semaphore_signal(round_sem.at[i], inc=1, device_id=target, device_id_type=MESH)

    factor_loads = [
        pltpu.make_async_copy(slot_in, slot_ref, factor_sem.at[0]),
        pltpu.make_async_copy(day_in, day_ref, factor_sem.at[1]),
    ]
    for copy in factor_loads:
        copy.start()

    def target_x(j):
        return lax.rem(x + jnp.where(j == 0, 2, jnp.where(j == 1, 1, jnp.where(j == 2, 3, 0))), NX)

    def load_copy(chunk):
        lanes = pl.ds(pl.multiple_of(chunk * STRIDE, R), WINDOW)
        return pltpu.make_async_copy(traffic.at[:, :, lanes], t_win.at[chunk], load_sem.at[chunk])

    def load_step(j, carry):
        load_copy(chunk_of(target_x(j), 1 - core)).start()
        load_copy(chunk_of(target_x(j), core)).start()
        return carry

    lax.fori_loop(0, NX, load_step, 0)

    for c in range(GROUP):
        if c:
            gathered[c, 0 : SHIFT * c] = jnp.zeros((SHIFT * c, R), f32)
        if SHIFT * c + own < WINDOW:
            gathered[c, SHIFT * c + own :] = jnp.zeros((WINDOW - own - SHIFT * c, R), f32)
    c_wide[...] = jnp.zeros_like(c_wide)
    c_low[...] = jnp.zeros_like(c_low)
    for copy in factor_loads:
        copy.wait()

    slot_local = slot_ref[pl.ds(pl.multiple_of(slot_index * slots, 8), slots), :]
    khatri = [slot_local * day_ref[pl.ds(day_index * days + k, 1), :] for k in range(days)]
    khatri = jnp.concatenate(khatri + [jnp.zeros((padded - rows, R), f32)], axis=0)
    w_high, w_low = split(khatri)
    w_cat[:, 0:R] = w_high
    w_cat[:, R:] = w_low

    half = own // 2

    def rows_of(chunk):
        return pl.ds(pl.multiple_of(chunk * SHIFT, SHIFT), own)

    def half_rows_of(chunk, h):
        return pl.ds(pl.multiple_of(chunk * SHIFT + h * half, 8), half)

    def first_product(chunk, target):
        load_copy(chunk).wait()
        block = [t_win[chunk, k] for k in range(days)] + [jnp.zeros((padded - rows, WINDOW), f32)]
        high, low = split(jnp.concatenate(block, axis=0))
        t_high[chunk] = high
        t_low[chunk] = low
        wide = dot(high, w_cat[...], ((0,), (0,)))
        target[...] = wide[:, 0:R] + wide[:, R:] + dot(low, w_cat[:, 0:R], ((0,), (0,)))

    def sibling_copy(j):
        chunk = chunk_of(target_x(j), 1 - core)
        return pltpu.make_async_remote_copy(
            src_ref=win_sib.at[j].at[rows_of(chunk)], dst_ref=sib_recv.at[j],
            send_sem=sib_ssem.at[j], recv_sem=sib_rsem.at[j],
            device_id=device(z, y, x, 1 - core), device_id_type=MESH,
        )

    def x_copy(j, h):
        rows_h = pl.ds(pl.multiple_of(h * half, 8), half)
        return pltpu.make_async_remote_copy(
            src_ref=x_send.at[j].at[rows_h], dst_ref=x_recv.at[j].at[rows_h],
            send_sem=x_ssem.at[j, h], recv_sem=x_rsem.at[j, h],
            device_id=device(z, y, target_x(j), core), device_id_type=MESH,
        )

    def scatter_step(j, carry):
        @pl.when(j < NX)
        def _():
            first_product(chunk_of(target_x(j), 1 - core), win_sib.at[j])
            first_product(chunk_of(target_x(j), core), win_own.at[j])

            @pl.when(j == 0)
            def _():
                pl.semaphore_wait(barrier, barrier_count)
                round_z(0)

            sibling_copy(j).start()

        @pl.when(j > 0)
        def _():
            sibling_copy(j - 1).wait_recv()
            x_send[j - 1] = win_own[j - 1, rows_of(chunk_of(target_x(j - 1), core)), :] + sib_recv[j - 1]

            @pl.when(j < NX)
            def _():
                x_copy(j - 1, 0).start()

        return carry

    lax.fori_loop(0, NX + 1, scatter_step, 0)
    for j in range(NX - 1):
        x_copy(j, 1).start()

    pl.semaphore_wait(round_sem.at[0], 2)
    round_z(1)
    gram_day = gram_of(day_ref[...])
    inv_sensor = inverse(regularize(gram_of(slot_ref[...]) * gram_day))

    def own_half(h):
        total = x_send[NX - 1, h * half : (h + 1) * half]
        for j in range(NX - 1):
            x_copy(j, h).wait_recv()
            total = total + x_recv[j, h * half : (h + 1) * half]
        sensor_raw = dot(total, inv_sensor, precision=highest)
        gathered[me, half_rows_of(me, h), :] = sensor_raw
        return gram_of(sensor_raw)

    def device_y(p):
        return device(z, p, x, core)

    def device_z(p):
        return device(p, y, x, core)

    def device_32(p):
        return (z * NY + p // 8, lax.rem(p // 2, 4), lax.rem(p, 2))

    me_32 = y * 8 + me
    gx = Exchange((gx_buf, gx_s, gx_r), GROUP, me, group_device, gram_part)
    gy = Exchange((gy_buf, gy_s, gy_r), NY, y, device_y, gram_rows)
    gz = Exchange((gz_buf, gz_s, gz_r), NZ, z, device_z)
    ga = Exchange((ga_buf, ga_s, ga_r), 32, me_32, device_32)

    def source_x(j):
        return lax.rem(x + jnp.where(j == 0, 2, jnp.where(j == 1, 3, jnp.where(j == 2, 1, 0))), NX)

    def gather_copy(j, h, sender=False):
        chunk = me if sender else chunk_of(source_x(j), core)
        place = gathered.at[chunk].at[half_rows_of(chunk, h)]
        return pltpu.make_async_remote_copy(
            src_ref=place, dst_ref=place, send_sem=gat_ssem.at[j, h], recv_sem=gat_rsem.at[j, h],
            device_id=device(z, y, target_x(j), core), device_id_type=MESH,
        )

    def forward_copy(j, h, sender=False):
        chunk = chunk_of(source_x(j), core if sender else 1 - core)
        place = gathered.at[chunk].at[half_rows_of(chunk, h)]
        return pltpu.make_async_remote_copy(
            src_ref=place, dst_ref=place, send_sem=fwd_ssem.at[j, h], recv_sem=fwd_rsem.at[j, h],
            device_id=device(z, y, x, 1 - core), device_id_type=MESH,
        )

    def gather_start(h):
        for j in (1, 2, 0):
            gather_copy(j, h, True).start()
        forward_copy(3, h, True).start()

    pl.semaphore_wait(round_sem.at[1], 2)
    round_z(2)
    gram = own_half(0)
    gather_start(0)
    gram = gram + own_half(1)
    for i in range(GROUP):
        gram_part[i] = gram[16 * i : 16 * i + 16]
    gx.start()
    gx_buf[me] = gram_part[me]
    gather_start(1)
    pl.semaphore_wait(round_sem.at[2], 2)

    def second_product(chunk):
        high, low = split(gathered[chunk])
        c_wide[...] += dot(t_high[chunk], jnp.concatenate([high, low], axis=1))
        c_low[...] += dot(t_low[chunk], high)

    def own_core(j):
        second_product(chunk_of(source_x(j), core))

    def other_core(j):
        forward_copy(j, 0).wait_recv()
        forward_copy(j, 1).wait_recv()
        second_product(chunk_of(source_x(j), 1 - core))

    def pass_on(j, h):
        gather_copy(j, h).wait_recv()
        forward_copy(j, h, True).start()

    def gather_step(i, carry):
        @pl.when(i == 0)
        def _():
            own_core(3)
            other_core(3)
            pass_on(1, 0)
            pass_on(2, 0)
            pass_on(0, 0)
            gx.wait_recv()
            gram = gx.total()
            for i in range(NY):
                gram_rows[i] = gram[4 * i : 4 * i + 4]
            gy.start()
            gy_buf[y] = gram_rows[y]
            pass_on(1, 1)
            pass_on(2, 1)

        @pl.when(i == 3)
        def _():
            pass_on(0, 1)

        j = jnp.where(i == 0, 1, jnp.where(i == 1, 2, 0))

        @pl.when(i != 2)
        def _():
            own_core(j)

        @pl.when(i == 2)
        def _():
            gy.wait_recv()
            gz_buf[z] = gy.total()
            gz.start()

        @pl.when(i >= 2)
        def _():
            other_core(jnp.where(i == 2, 1, 0))

        @pl.when(i == 2)
        def _():
            other_core(2)

        return carry

    lax.fori_loop(0, NX, gather_step, 0)

    contracted = c_wide[:, 0:R] + c_wide[:, R:] + c_low[...]
    contracted = [contracted[k * slots : (k + 1) * slots] for k in range(days)]
    part = contracted[0] * day_ref[pl.ds(day_index * days, 1), :]
    for k in range(1, days):
        part = part + contracted[k] * day_ref[pl.ds(day_index * days + k, 1), :]
    piece = slots // 8
    for i in range(8):
        slot_part[i] = part[i * piece : (i + 1) * piece]

    def device_8(p):
        return device(z, p // 2, x_hi * 2 + lax.rem(p, 2), core)

    me_8 = y * 2 + day_index
    s8 = Exchange((s8_buf, s8_s, s8_r), 8, me_8, device_8, slot_part)
    sz = Exchange((sz_buf, sz_s, sz_r), NZ, z, device_z)
    sa = Exchange((sa_buf, sa_s, sa_r), 32, me_32, device_32)
    s8.start()
    s8_buf[me_8] = slot_part[me_8]

    for p in range(NY):
        for k in range(days):
            for m in range(strips):
                row = (p * strips + m) * strip
                con_part[p, k * strips + m] = contracted[k][row : row + strip]
        for i in range(days * strips, NZ):
            con_part[p, i] = jnp.zeros((strip, R), f32)
    cy = Exchange((cy_buf, cy_s, cy_r), NY, y, device_y, con_part)
    cz = Exchange((cz_buf, cz_s, cz_r), NZ, z, device_z, con_rows)
    ca = Exchange((ca_buf, ca_s, ca_r), NZ, z, device_z)
    cy.start()
    cy_buf[y] = con_part[y]

    s8.wait_recv()
    sz_buf[z] = s8.total()
    sz.start()

    cy.wait_recv()
    con_rows[...] = cy.total()
    cz.start()
    cz_buf[z] = con_rows[z]

    gz.wait_recv()
    ga_buf[me_32] = gz.total()
    ga.start()
    sz.wait_recv()
    sa_buf[me_32] = sz.total()
    sa.start()
    cz.wait_recv()
    ca_buf[z] = cz.total()
    ca.start()
    ga.wait_recv()
    gram = jnp.concatenate([ga_buf[i * GROUP + g] for g in range(GROUP) for i in range(NY)], axis=0)

    def norms_of(gram, count):
        square = jnp.where(diagonal_mask(), gram, 0.0)
        row = jnp.sqrt(jnp.sum(square, axis=0, keepdims=True) / count + epsilon)
        column = jnp.sqrt(jnp.sum(square, axis=1, keepdims=True) / count + epsilon)
        return row, gram / (column * row)

    sensor_norms, gram_sensor = norms_of(gram, sensor_count)
    sensor_out[...] = gathered[me, rows_of(me), :] / sensor_norms
    inv_slot = inverse(regularize(gram_sensor * gram_day))

    sa.wait_recv()
    slot_rhs = [sa_buf[(i // 2) * 8 + s * 2 + i % 2] for s in range(4) for i in range(8)]
    slot_rhs = jnp.concatenate(slot_rhs, axis=0) / sensor_norms
    slot_all[...] = dot(slot_rhs, inv_slot, precision=highest)
    gram = gram_of(slot_all[...])
    slot_norms, gram_slot_new = norms_of(gram, slot_count)
    slot_new = slot_all[pl.ds(pl.multiple_of(slot_index * slots, 8), slots), :] / slot_norms
    slot_out[...] = slot_new

    weight = slot_new / sensor_norms
    for i in range(NY * strips):
        weights[i] = weight[i * strip : (i + 1) * strip]
    ca.wait_recv()
    for k in range(days):
        total = ca_buf[k * strips] * weights[y * strips]
        for m in range(1, strips):
            total = total + ca_buf[k * strips + m] * weights[y * strips + m]
        dy_buf[y * 4 + slot_index, k : k + 1] = jnp.sum(total, axis=0, keepdims=True)

    def device_16(p):
        return (z * NY + p // 4, lax.rem(p, 4), day_index)

    me_16 = y * 4 + slot_index
    dy = Exchange((dy_buf, dy_s, dy_r), 16, me_16, device_16)
    dy.start()
    inv_day = inverse(regularize(gram_sensor * gram_slot_new))
    dy.wait_recv()
    day_out[...] = dot(dy.total(), inv_day, precision=highest)

    def drain(j, carry):
        sibling_copy(j).wait_send()
        for h in range(2):
            forward_copy(j, h, True).wait_send()

        @pl.when(j < NX - 1)
        def _():
            for h in range(2):
                x_copy(j, h).wait_send()
                gather_copy(j, h, True).wait_send()

        return carry

    lax.fori_loop(0, NX, drain, 0)
    for exchange in (gx, gy, gz, ga, s8, sz, sa, cy, cz, ca, dy):
        exchange.wait_send()


def on_device(traffic, slot_factor, day_factor):
    days, slots, sensors = traffic.shape
    slot_count = slot_factor.shape[0]
    sensor_count = sensors * lax.axis_size("sensor")
    own = sensors // GROUP
    padded = (days * slots + 15) // 16 * 16
    strip = slots // NY // (NZ // days)

    def exchange_scratch(count, *block):
        return [
            pltpu.VMEM((count, *block), f32),
            pltpu.SemaphoreType.DMA((count,)),
            pltpu.SemaphoreType.DMA((count,)),
        ]

    dma = pltpu.SemaphoreType.DMA
    scratch = [
        pltpu.VMEM(slot_factor.shape, f32),
        pltpu.VMEM(day_factor.shape, f32),
        pltpu.VMEM((GROUP, days, slots, WINDOW), f32),
        pltpu.VMEM((GROUP, padded, WINDOW), bf16),
        pltpu.VMEM((GROUP, padded, WINDOW), bf16),
        pltpu.VMEM((padded, 2 * R), bf16),
        dma((2,)),
        dma((GROUP,)),
        pltpu.SemaphoreType.REGULAR((3,)),
        pltpu.VMEM((NX, WINDOW, R), f32),
        pltpu.VMEM((NX, WINDOW, R), f32),
        *exchange_scratch(NX, own, R),
        pltpu.VMEM((NX, own, R), f32),
        pltpu.VMEM((NX - 1, own, R), f32),
        dma((NX - 1, 2)), dma((NX - 1, 2)),
        pltpu.VMEM((GROUP, WINDOW, R), f32),
        dma((NX - 1, 2)), dma((NX - 1, 2)), dma((NX, 2)), dma((NX, 2)),
        pltpu.VMEM((padded, 2 * R), f32),
        pltpu.VMEM((padded, R), f32),
        pltpu.VMEM((GROUP, 16, R), f32),
        pltpu.VMEM((NY, 4, R), f32),
        *exchange_scratch(GROUP, 16, R),
        *exchange_scratch(NY, 4, R),
        *exchange_scratch(NZ, 4, R),
        *exchange_scratch(32, 4, R),
        pltpu.VMEM((8, slots // 8, R), f32),
        *exchange_scratch(8, slots // 8, R),
        *exchange_scratch(NZ, slots // 8, R),
        *exchange_scratch(32, slots // 8, R),
        pltpu.VMEM(slot_factor.shape, f32),
        pltpu.VMEM((NY, NZ, strip, R), f32),
        pltpu.VMEM((NZ, strip, R), f32),
        *exchange_scratch(NY, NZ, strip, R),
        *exchange_scratch(NZ, strip, R),
        *exchange_scratch(NZ, strip, R),
        pltpu.VMEM((slots // strip, strip, R), f32),
        *exchange_scratch(16, days, R),
    ]
    vmem = pl.BlockSpec(memory_space=pltpu.VMEM)

    def kernel(*refs):
        body(sensor_count, slot_count, *refs)

    results = pl.pallas_call(
        kernel,
        out_shape=(
            jax.ShapeDtypeStruct((own, R), f32),
            jax.ShapeDtypeStruct((slots, R), f32),
            jax.ShapeDtypeStruct((days, R), f32),
        ),
        in_specs=[pl.BlockSpec(memory_space=pltpu.HBM)] * 3,
        out_specs=(vmem, vmem, vmem),
        scratch_shapes=scratch,
        compiler_params=pltpu.CompilerParams(
            collective_id=0, has_side_effects=True, vmem_limit_bytes=60 * 1024 * 1024
        ),
    )(traffic, slot_factor, day_factor)

    def store(*refs):
        for i in range(3):
            refs[3 + i][...] = refs[i][...]

    return pl.pallas_call(
        store,
        out_shape=tuple(jax.ShapeDtypeStruct(a.shape, f32) for a in results),
        in_specs=[vmem] * 3,
        out_specs=(vmem,) * 3,
    )(*results)


def solution(mesh):
    in_specs = (P("day", "slot", "sensor"), P(), P())
    out_specs = (P(("sensor", "slot", "day"), None), P("slot", None), P("day", None))
    return jax.shard_map(
        on_device, mesh=mesh, in_specs=in_specs, out_specs=out_specs, check_vma=False
    )
```

```python
import jax
import jax.numpy as jnp
from jax import lax
from jax.experimental import pallas as pl
from jax.experimental.pallas import tpu as pltpu
from jax.sharding import PartitionSpec as P

MESH = pl.DeviceIdType.MESH
highest = lax.Precision.HIGHEST
f32 = jnp.float32
bf16 = jnp.bfloat16
ridge_scale = 0.001
epsilon = 1e-05

R = 128
NX, NY, NZ = 4, 4, 16
GROUP = 8
WINDOW, STRIDE, SHIFT = 512, 384, 16


def dot(a, b, contract=((1,), (0,)), precision=None):
    return lax.dot_general(a, b, (contract, ((), ())), precision=precision, preferred_element_type=f32)


def gram_of(rows):
    return dot(rows, rows, ((0,), (0,)), highest)


def diagonal_mask():
    return lax.broadcasted_iota(jnp.int32, (R, R), 0) == lax.broadcasted_iota(jnp.int32, (R, R), 1)


def regularize(matrix):
    eye = diagonal_mask()
    mean = jnp.sum(jnp.where(eye, matrix, 0.0)) / R
    return matrix + jnp.where(eye, ridge_scale * mean, 0.0)


def inverse(matrix):
    lane = lax.broadcasted_iota(jnp.int32, (8, R), 1)
    sub = lax.broadcasted_iota(jnp.int32, (8, R), 0)
    lane_rest = lax.broadcasted_iota(jnp.int32, (R - 8, R), 1)

    def step(_, matrix):
        top, rest = matrix[0:8], matrix[8:]
        rows = [jnp.broadcast_to(top[i : i + 1, :], (8, R)) for i in range(8)]
        a = {(i, j): jnp.broadcast_to(rows[i][:, j : j + 1], (8, R)) for i in range(8) for j in range(i, 8)}
        rows = [jnp.where(lane == i, 1.0, jnp.where(lane < 8, 0.0, rows[i])) for i in range(8)]
        lower, scale = {}, []
        for t in range(8):
            scale.append(1.0 / a[t, t])
            for s in range(t + 1, 8):
                lower[s, t] = a[t, s] * scale[t]
            for s in range(t + 1, 8):
                for u in range(s, 8):
                    a[s, u] = a[s, u] - lower[s, t] * a[t, u]
                rows[s] = rows[s] - lower[s, t] * rows[t]
        rows = [rows[t] * scale[t] for t in range(8)]
        for t in range(7, -1, -1):
            for s in range(t):
                rows[s] = rows[s] - lower[t, s] * rows[t]
        new_top = rows[7]
        for i in range(7):
            new_top = jnp.where(sub == i, rows[i], new_top)
        base = jnp.where(lane_rest < 8, 0.0, rest)
        for i in range(8):
            base = base - rest[:, i : i + 1] * rows[i][0:1, :]
        return pltpu.roll(jnp.concatenate([base, new_top], axis=0), R - 8, 1)

    return lax.fori_loop(0, R // 8, step, matrix)


def split(value):
    high = value.astype(bf16)
    return high, (value - high.astype(f32)).astype(bf16)


class Exchange:
    def __init__(self, refs, count, me, device, source=None):
        self.buffer, self.send_sem, self.recv_sem = refs
        self.count, self.me, self.device, self.source = count, me, device, source

    def start(self):
        middle = self.count // 2
        for i in range(self.count - 1):
            k = middle + (i + 1) // 2 if i % 2 else middle - i // 2
            peer = lax.rem(self.me + k, self.count)
            source = self.buffer.at[self.me] if self.source is None else self.source.at[peer]
            pltpu.make_async_remote_copy(
                src_ref=source, dst_ref=self.buffer.at[self.me],
                send_sem=self.send_sem, recv_sem=self.recv_sem,
                device_id=self.device(peer), device_id_type=MESH,
            ).start()

    def all_copies(self):
        part = self.buffer.at[pl.ds(0, self.count - 1)]
        return pltpu.make_async_remote_copy(
            src_ref=part, dst_ref=part, send_sem=self.send_sem, recv_sem=self.recv_sem,
            device_id=self.device(lax.rem(self.me + 1, self.count)), device_id_type=MESH,
        )

    def wait_recv(self):
        self.all_copies().wait_recv()

    def wait_send(self):
        self.all_copies().wait_send()

    def total(self):
        total = self.buffer[0]
        for i in range(1, self.count):
            total = total + self.buffer[i]
        return total


def body(
    sensor_count, slot_count,
    traffic, slot_in, day_in, sensor_out, slot_out, day_out,
    slot_ref, day_ref, t_win, t_high, t_low, w_cat, factor_sem, load_sem, round_sem,
    sensor_stage, slot_stage, day_stage, out_sem,
    win_sib, win_own, sib_recv, sib_ssem, sib_rsem, x_send, x_recv, x_ssem, x_rsem,
    gathered, gat_ssem, gat_rsem, fwd_ssem, fwd_rsem,
    c_wide, c_low,
    gram_part, gram_rows, gx_buf, gx_s, gx_r, gy_buf, gy_s, gy_r, gz_buf, gz_s, gz_r, ga_buf, ga_s, ga_r,
    slot_part, s8_buf, s8_s, s8_r, sz_buf, sz_s, sz_r, sa_buf, sa_s, sa_r, slot_all,
    con_part, con_rows, cy_buf, cy_s, cy_r, cz_buf, cz_s, cz_r, ca_buf, ca_s, ca_r, weights,
    dy_buf, dy_s, dy_r,
):
    days, slots, sensors = traffic.shape
    rows = days * slots
    padded = w_cat.shape[0]
    strips = NZ // days
    strip = slots // NY // strips
    own = sensors // GROUP
    sensor_index = lax.axis_index("sensor")
    slot_index = lax.axis_index("slot")
    day_index = lax.axis_index("day")
    z, y = sensor_index // NY, lax.rem(sensor_index, NY)
    core = lax.rem(slot_index, 2)
    x_hi = slot_index // 2
    x = x_hi * 2 + day_index

    def device(z, y, x, core):
        return (z * NY + y, (x // 2) * 2 + core, lax.rem(x, 2))

    def chunk_of(x, core):
        return ((x // 2) * 2 + core) * 2 + lax.rem(x, 2)

    def group_device(index):
        return (sensor_index, index // 2, lax.rem(index, 2))

    me = chunk_of(x, core)

    barrier = pltpu.get_barrier_semaphore()

    def greet(target):
        pl.semaphore_signal(barrier, inc=1, device_id=target, device_id_type=MESH)

    def greet_group(k, carry):
        greet(group_device(lax.rem(me + k, GROUP)))
        return carry

    lax.fori_loop(1, GROUP, greet_group, 0)
    for k in range(1, NY):
        greet(device(z, lax.rem(y + k, NY), x, core))
    for k in (1, NZ - 1):
        greet(device(lax.rem(z + k, NZ), y, x, core))
    barrier_count = (GROUP - 1) + (NY - 1) + 2

    def round_z(i):
        for k in (2**i, NZ - 2**i):
            target = device(lax.rem(z + k, NZ), y, x, core)
            pl.semaphore_signal(round_sem.at[i], inc=1, device_id=target, device_id_type=MESH)

    out_copies = [
        pltpu.make_async_copy(source, target, out_sem.at[i])
        for i, (source, target) in enumerate(((sensor_stage, sensor_out), (slot_stage, slot_out), (day_stage, day_out)))
    ]
    factor_loads = [
        pltpu.make_async_copy(slot_in, slot_ref, factor_sem.at[0]),
        pltpu.make_async_copy(day_in, day_ref, factor_sem.at[1]),
    ]
    for copy in factor_loads:
        copy.start()

    def target_x(j):
        return lax.rem(x + jnp.where(j == 0, 2, jnp.where(j == 1, 1, jnp.where(j == 2, 3, 0))), NX)

    def load_copy(chunk):
        lanes = pl.ds(pl.multiple_of(chunk * STRIDE, R), WINDOW)
        return pltpu.make_async_copy(traffic.at[:, :, lanes], t_win.at[chunk], load_sem.at[chunk])

    def load_step(j, carry):
        load_copy(chunk_of(target_x(j), 1 - core)).start()
        load_copy(chunk_of(target_x(j), core)).start()
        return carry

    lax.fori_loop(0, NX, load_step, 0)

    for c in range(GROUP):
        if c:
            gathered[c, 0 : SHIFT * c] = jnp.zeros((SHIFT * c, R), f32)
        if SHIFT * c + own < WINDOW:
            gathered[c, SHIFT * c + own :] = jnp.zeros((WINDOW - own - SHIFT * c, R), f32)
    c_wide[...] = jnp.zeros_like(c_wide)
    c_low[...] = jnp.zeros_like(c_low)
    for copy in factor_loads:
        copy.wait()

    slot_local = slot_ref[pl.ds(pl.multiple_of(slot_index * slots, 8), slots), :]
    khatri = [slot_local * day_ref[pl.ds(day_index * days + k, 1), :] for k in range(days)]
    khatri = jnp.concatenate(khatri + [jnp.zeros((padded - rows, R), f32)], axis=0)
    w_high, w_low = split(khatri)
    w_cat[:, 0:R] = w_high
    w_cat[:, R:] = w_low

    half = own // 2

    def rows_of(chunk):
        return pl.ds(pl.multiple_of(chunk * SHIFT, SHIFT), own)

    def half_rows_of(chunk, h):
        return pl.ds(pl.multiple_of(chunk * SHIFT + h * half, 8), half)

    def first_product(chunk, target):
        load_copy(chunk).wait()
        block = [t_win[chunk, k] for k in range(days)] + [jnp.zeros((padded - rows, WINDOW), f32)]
        high, low = split(jnp.concatenate(block, axis=0))
        t_high[chunk] = high
        t_low[chunk] = low
        wide = dot(high, w_cat[...], ((0,), (0,)))
        target[...] = wide[:, 0:R] + wide[:, R:] + dot(low, w_cat[:, 0:R], ((0,), (0,)))

    def sibling_copy(j):
        chunk = chunk_of(target_x(j), 1 - core)
        return pltpu.make_async_remote_copy(
            src_ref=win_sib.at[j].at[rows_of(chunk)], dst_ref=sib_recv.at[j],
            send_sem=sib_ssem.at[j], recv_sem=sib_rsem.at[j],
            device_id=device(z, y, x, 1 - core), device_id_type=MESH,
        )

    def x_copy(j, h):
        rows_h = pl.ds(pl.multiple_of(h * half, 8), half)
        return pltpu.make_async_remote_copy(
            src_ref=x_send.at[j].at[rows_h], dst_ref=x_recv.at[j].at[rows_h],
            send_sem=x_ssem.at[j, h], recv_sem=x_rsem.at[j, h],
            device_id=device(z, y, target_x(j), core), device_id_type=MESH,
        )

    def scatter_step(j, carry):
        @pl.when(j < NX)
        def _():
            first_product(chunk_of(target_x(j), 1 - core), win_sib.at[j])
            first_product(chunk_of(target_x(j), core), win_own.at[j])

            @pl.when(j == 0)
            def _():
                pl.semaphore_wait(barrier, barrier_count)
                round_z(0)

            sibling_copy(j).start()

        @pl.when(j > 0)
        def _():
            sibling_copy(j - 1).wait_recv()
            x_send[j - 1] = win_own[j - 1, rows_of(chunk_of(target_x(j - 1), core)), :] + sib_recv[j - 1]

            @pl.when(j < NX)
            def _():
                x_copy(j - 1, 0).start()

        return carry

    lax.fori_loop(0, NX + 1, scatter_step, 0)
    for j in range(NX - 1):
        x_copy(j, 1).start()

    pl.semaphore_wait(round_sem.at[0], 2)
    round_z(1)
    gram_day = gram_of(day_ref[...])
    inv_sensor = inverse(regularize(gram_of(slot_ref[...]) * gram_day))

    def own_half(h):
        total = x_send[NX - 1, h * half : (h + 1) * half]
        for j in range(NX - 1):
            x_copy(j, h).wait_recv()
            total = total + x_recv[j, h * half : (h + 1) * half]
        sensor_raw = dot(total, inv_sensor, precision=highest)
        gathered[me, half_rows_of(me, h), :] = sensor_raw
        return gram_of(sensor_raw)

    def device_y(p):
        return device(z, p, x, core)

    def device_z(p):
        return device(p, y, x, core)

    def device_32(p):
        return (z * NY + p // 8, lax.rem(p // 2, 4), lax.rem(p, 2))

    me_32 = y * 8 + me
    gx = Exchange((gx_buf, gx_s, gx_r), GROUP, me, group_device, gram_part)
    gy = Exchange((gy_buf, gy_s, gy_r), NY, y, device_y, gram_rows)
    gz = Exchange((gz_buf, gz_s, gz_r), NZ, z, device_z)
    ga = Exchange((ga_buf, ga_s, ga_r), 32, me_32, device_32)

    def source_x(j):
        return lax.rem(x + jnp.where(j == 0, 2, jnp.where(j == 1, 3, jnp.where(j == 2, 1, 0))), NX)

    def gather_copy(j, h, sender=False):
        chunk = me if sender else chunk_of(source_x(j), core)
        place = gathered.at[chunk].at[half_rows_of(chunk, h)]
        return pltpu.make_async_remote_copy(
            src_ref=place, dst_ref=place, send_sem=gat_ssem.at[j, h], recv_sem=gat_rsem.at[j, h],
            device_id=device(z, y, target_x(j), core), device_id_type=MESH,
        )

    def forward_copy(j, h, sender=False):
        chunk = chunk_of(source_x(j), core if sender else 1 - core)
        place = gathered.at[chunk].at[half_rows_of(chunk, h)]
        return pltpu.make_async_remote_copy(
            src_ref=place, dst_ref=place, send_sem=fwd_ssem.at[j, h], recv_sem=fwd_rsem.at[j, h],
            device_id=device(z, y, x, 1 - core), device_id_type=MESH,
        )

    def gather_start(h):
        for j in (1, 2, 0):
            gather_copy(j, h, True).start()
        forward_copy(3, h, True).start()

    pl.semaphore_wait(round_sem.at[1], 2)
    round_z(2)
    gram = own_half(0)
    gather_start(0)
    gram = gram + own_half(1)
    for i in range(GROUP):
        gram_part[i] = gram[16 * i : 16 * i + 16]
    gx.start()
    gx_buf[me] = gram_part[me]
    gather_start(1)
    pl.semaphore_wait(round_sem.at[2], 2)

    def second_product(chunk):
        high, low = split(gathered[chunk])
        c_wide[...] += dot(t_high[chunk], jnp.concatenate([high, low], axis=1))
        c_low[...] += dot(t_low[chunk], high)

    def own_core(j):
        second_product(chunk_of(source_x(j), core))

    def other_core(j):
        forward_copy(j, 0).wait_recv()
        forward_copy(j, 1).wait_recv()
        second_product(chunk_of(source_x(j), 1 - core))

    def pass_on(j, h):
        gather_copy(j, h).wait_recv()
        forward_copy(j, h, True).start()

    def gather_step(i, carry):
        @pl.when(i == 0)
        def _():
            own_core(3)
            other_core(3)
            pass_on(1, 0)
            pass_on(2, 0)
            pass_on(0, 0)
            gx.wait_recv()
            gram = gx.total()
            for i in range(NY):
                gram_rows[i] = gram[4 * i : 4 * i + 4]
            gy.start()
            gy_buf[y] = gram_rows[y]
            pass_on(1, 1)
            pass_on(2, 1)

        @pl.when(i == 3)
        def _():
            pass_on(0, 1)

        j = jnp.where(i == 0, 1, jnp.where(i == 1, 2, 0))

        @pl.when(i != 2)
        def _():
            own_core(j)

        @pl.when(i == 2)
        def _():
            gy.wait_recv()
            gz_buf[z] = gy.total()
            gz.start()

        @pl.when(i >= 2)
        def _():
            other_core(jnp.where(i == 2, 1, 0))

        @pl.when(i == 2)
        def _():
            other_core(2)

        return carry

    lax.fori_loop(0, NX, gather_step, 0)

    contracted = c_wide[:, 0:R] + c_wide[:, R:] + c_low[...]
    contracted = [contracted[k * slots : (k + 1) * slots] for k in range(days)]
    part = contracted[0] * day_ref[pl.ds(day_index * days, 1), :]
    for k in range(1, days):
        part = part + contracted[k] * day_ref[pl.ds(day_index * days + k, 1), :]
    piece = slots // 8
    for i in range(8):
        slot_part[i] = part[i * piece : (i + 1) * piece]

    def device_8(p):
        return device(z, p // 2, x_hi * 2 + lax.rem(p, 2), core)

    me_8 = y * 2 + day_index
    s8 = Exchange((s8_buf, s8_s, s8_r), 8, me_8, device_8, slot_part)
    sz = Exchange((sz_buf, sz_s, sz_r), NZ, z, device_z)
    sa = Exchange((sa_buf, sa_s, sa_r), 32, me_32, device_32)
    s8.start()
    s8_buf[me_8] = slot_part[me_8]

    for p in range(NY):
        for k in range(days):
            for m in range(strips):
                row = (p * strips + m) * strip
                con_part[p, k * strips + m] = contracted[k][row : row + strip]
        for i in range(days * strips, NZ):
            con_part[p, i] = jnp.zeros((strip, R), f32)
    cy = Exchange((cy_buf, cy_s, cy_r), NY, y, device_y, con_part)
    cz = Exchange((cz_buf, cz_s, cz_r), NZ, z, device_z, con_rows)
    ca = Exchange((ca_buf, ca_s, ca_r), NZ, z, device_z)
    cy.start()
    cy_buf[y] = con_part[y]

    for j in range(NX):
        sibling_copy(j).wait_send()
        for h in range(2):
            forward_copy(j, h, True).wait_send()
            if j < NX - 1:
                x_copy(j, h).wait_send()
                gather_copy(j, h, True).wait_send()
    gx.wait_send()
    gy.wait_send()

    s8.wait_recv()
    sz_buf[z] = s8.total()
    sz.start()

    cy.wait_recv()
    con_rows[...] = cy.total()
    cz.start()
    cz_buf[z] = con_rows[z]

    gz.wait_recv()
    ga_buf[me_32] = gz.total()
    ga.start()
    for exchange in (gz, s8, cy, sz):
        exchange.wait_send()
    sz.wait_recv()
    sa_buf[me_32] = sz.total()
    sa.start()
    ga.wait_recv()
    gram = jnp.concatenate([ga_buf[i * GROUP + g] for g in range(GROUP) for i in range(NY)], axis=0)

    def norms_of(gram, count):
        square = jnp.where(diagonal_mask(), gram, 0.0)
        row = jnp.sqrt(jnp.sum(square, axis=0, keepdims=True) / count + epsilon)
        column = jnp.sqrt(jnp.sum(square, axis=1, keepdims=True) / count + epsilon)
        return row, gram / (column * row)

    sensor_norms, gram_sensor = norms_of(gram, sensor_count)
    sensor_stage[...] = gathered[me, rows_of(me), :] / sensor_norms
    out_copies[0].start()
    cz.wait_recv()
    ca_buf[z] = cz.total()
    ca.start()
    inv_slot = inverse(regularize(gram_sensor * gram_day))

    ga.wait_send()
    cz.wait_send()
    sa.wait_recv()
    slot_rhs = [sa_buf[(i // 2) * 8 + s * 2 + i % 2] for s in range(4) for i in range(8)]
    slot_rhs = jnp.concatenate(slot_rhs, axis=0) / sensor_norms
    slot_all[...] = dot(slot_rhs, inv_slot, precision=highest)
    gram = gram_of(slot_all[...])
    slot_norms, gram_slot_new = norms_of(gram, slot_count)
    slot_new = slot_all[pl.ds(pl.multiple_of(slot_index * slots, 8), slots), :] / slot_norms
    slot_stage[...] = slot_new
    out_copies[1].start()

    weight = slot_new / sensor_norms
    for i in range(NY * strips):
        weights[i] = weight[i * strip : (i + 1) * strip]
    sa.wait_send()
    ca.wait_recv()
    for k in range(days):
        total = ca_buf[k * strips] * weights[y * strips]
        for m in range(1, strips):
            total = total + ca_buf[k * strips + m] * weights[y * strips + m]
        dy_buf[y * 4 + slot_index, k : k + 1] = jnp.sum(total, axis=0, keepdims=True)

    def device_16(p):
        return (z * NY + p // 4, lax.rem(p, 4), day_index)

    me_16 = y * 4 + slot_index
    dy = Exchange((dy_buf, dy_s, dy_r), 16, me_16, device_16)
    dy.start()
    inv_day = inverse(regularize(gram_sensor * gram_slot_new))
    ca.wait_send()
    dy.wait_recv()
    day_stage[...] = dot(dy.total(), inv_day, precision=highest)
    out_copies[2].start()
    for copy in out_copies:
        copy.wait()

    dy.wait_send()


def on_device(traffic, slot_factor, day_factor):
    days, slots, sensors = traffic.shape
    slot_count = slot_factor.shape[0]
    sensor_count = sensors * lax.axis_size("sensor")
    own = sensors // GROUP
    padded = (days * slots + 15) // 16 * 16
    strip = slots // NY // (NZ // days)

    def exchange_scratch(count, *block):
        return [
            pltpu.VMEM((count, *block), f32),
            pltpu.SemaphoreType.DMA,
            pltpu.SemaphoreType.DMA,
        ]

    dma = pltpu.SemaphoreType.DMA
    scratch = [
        pltpu.VMEM(slot_factor.shape, f32),
        pltpu.VMEM(day_factor.shape, f32),
        pltpu.VMEM((GROUP, days, slots, WINDOW), f32),
        pltpu.VMEM((GROUP, padded, WINDOW), bf16),
        pltpu.VMEM((GROUP, padded, WINDOW), bf16),
        pltpu.VMEM((padded, 2 * R), bf16),
        dma((2,)),
        dma((GROUP,)),
        pltpu.SemaphoreType.REGULAR((3,)),
        pltpu.VMEM((own, R), f32),
        pltpu.VMEM((slots, R), f32),
        pltpu.VMEM((days, R), f32),
        dma((3,)),
        pltpu.VMEM((NX, WINDOW, R), f32),
        pltpu.VMEM((NX, WINDOW, R), f32),
        pltpu.VMEM((NX, own, R), f32),
        dma((NX,)), dma((NX,)),
        pltpu.VMEM((NX, own, R), f32),
        pltpu.VMEM((NX - 1, own, R), f32),
        dma((NX - 1, 2)), dma((NX - 1, 2)),
        pltpu.VMEM((GROUP, WINDOW, R), f32),
        dma((NX - 1, 2)), dma((NX - 1, 2)), dma((NX, 2)), dma((NX, 2)),
        pltpu.VMEM((padded, 2 * R), f32),
        pltpu.VMEM((padded, R), f32),
        pltpu.VMEM((GROUP, 16, R), f32),
        pltpu.VMEM((NY, 4, R), f32),
        *exchange_scratch(GROUP, 16, R),
        *exchange_scratch(NY, 4, R),
        *exchange_scratch(NZ, 4, R),
        *exchange_scratch(32, 4, R),
        pltpu.VMEM((8, slots // 8, R), f32),
        *exchange_scratch(8, slots // 8, R),
        *exchange_scratch(NZ, slots // 8, R),
        *exchange_scratch(32, slots // 8, R),
        pltpu.VMEM(slot_factor.shape, f32),
        pltpu.VMEM((NY, NZ, strip, R), f32),
        pltpu.VMEM((NZ, strip, R), f32),
        *exchange_scratch(NY, NZ, strip, R),
        *exchange_scratch(NZ, strip, R),
        *exchange_scratch(NZ, strip, R),
        pltpu.VMEM((slots // strip, strip, R), f32),
        *exchange_scratch(16, days, R),
    ]
    vmem = pl.BlockSpec(memory_space=pltpu.VMEM)

    def kernel(*refs):
        body(sensor_count, slot_count, *refs)

    results = pl.pallas_call(
        kernel,
        out_shape=(
            jax.ShapeDtypeStruct((own, R), f32),
            jax.ShapeDtypeStruct((slots, R), f32),
            jax.ShapeDtypeStruct((days, R), f32),
        ),
        in_specs=[pl.BlockSpec(memory_space=pltpu.HBM)] * 3,
        out_specs=(pl.BlockSpec(memory_space=pl.ANY),) * 3,
        scratch_shapes=scratch,
        compiler_params=pltpu.CompilerParams(
            collective_id=0, has_side_effects=True, vmem_limit_bytes=60 * 1024 * 1024
        ),
    )(traffic, slot_factor, day_factor)

    def store(*refs):
        for i in range(3):
            refs[3 + i][...] = refs[i][...]

    return pl.pallas_call(
        store,
        out_shape=tuple(jax.ShapeDtypeStruct(a.shape, f32) for a in results),
        in_specs=[vmem] * 3,
        out_specs=(vmem,) * 3,
    )(*results)


def solution(mesh):
    in_specs = (P("day", "slot", "sensor"), P(), P())
    out_specs = (P(("sensor", "slot", "day"), None), P("slot", None), P("day", None))
    return jax.shard_map(
        on_device, mesh=mesh, in_specs=in_specs, out_specs=out_specs, check_vma=False
    )
```

```python
import jax
import jax.numpy as jnp
from jax import lax
from jax.experimental import pallas as pl
from jax.experimental.pallas import tpu as pltpu
from jax.sharding import PartitionSpec as P

MESH = pl.DeviceIdType.MESH
highest = lax.Precision.HIGHEST
f32 = jnp.float32
bf16 = jnp.bfloat16
ridge_scale = 0.001
epsilon = 1e-05

R = 128
NX, NY, NZ = 4, 4, 16
GROUP = 8
WINDOW, STRIDE, SHIFT = 512, 384, 16


def dot(a, b, contract=((1,), (0,)), precision=None):
    return lax.dot_general(a, b, (contract, ((), ())), precision=precision, preferred_element_type=f32)


def gram_of(rows):
    return dot(rows, rows, ((0,), (0,)), highest)


def diagonal_mask():
    return lax.broadcasted_iota(jnp.int32, (R, R), 0) == lax.broadcasted_iota(jnp.int32, (R, R), 1)


def regularize(matrix):
    eye = diagonal_mask()
    mean = jnp.sum(jnp.where(eye, matrix, 0.0)) / R
    return matrix + jnp.where(eye, ridge_scale * mean, 0.0)


def inverse(matrix):
    lane = lax.broadcasted_iota(jnp.int32, (8, R), 1)
    sub = lax.broadcasted_iota(jnp.int32, (8, R), 0)
    lane_rest = lax.broadcasted_iota(jnp.int32, (R - 8, R), 1)

    def step(_, matrix):
        top, rest = matrix[0:8], matrix[8:]
        rows = [jnp.broadcast_to(top[i : i + 1, :], (8, R)) for i in range(8)]
        a = {(i, j): jnp.broadcast_to(rows[i][:, j : j + 1], (8, R)) for i in range(8) for j in range(i, 8)}
        rows = [jnp.where(lane == i, 1.0, jnp.where(lane < 8, 0.0, rows[i])) for i in range(8)]
        lower, scale = {}, []
        for t in range(8):
            scale.append(1.0 / a[t, t])
            for s in range(t + 1, 8):
                lower[s, t] = a[t, s] * scale[t]
            for s in range(t + 1, 8):
                for u in range(s, 8):
                    a[s, u] = a[s, u] - lower[s, t] * a[t, u]
                rows[s] = rows[s] - lower[s, t] * rows[t]
        rows = [rows[t] * scale[t] for t in range(8)]
        for t in range(7, -1, -1):
            for s in range(t):
                rows[s] = rows[s] - lower[t, s] * rows[t]
        new_top = rows[7]
        for i in range(7):
            new_top = jnp.where(sub == i, rows[i], new_top)
        base = jnp.where(lane_rest < 8, 0.0, rest)
        for i in range(8):
            base = base - rest[:, i : i + 1] * rows[i][0:1, :]
        return pltpu.roll(jnp.concatenate([base, new_top], axis=0), R - 8, 1)

    return lax.fori_loop(0, R // 8, step, matrix)


def split(value):
    high = value.astype(bf16)
    return high, (value - high.astype(f32)).astype(bf16)


class Exchange:
    def __init__(self, refs, count, me, device, source=None):
        self.buffer, self.send_sem, self.recv_sem = refs
        self.count, self.me, self.device, self.source = count, me, device, source

    def start(self):
        middle = self.count // 2
        for i in range(self.count - 1):
            k = middle + (i + 1) // 2 if i % 2 else middle - i // 2
            peer = lax.rem(self.me + k, self.count)
            source = self.buffer.at[self.me] if self.source is None else self.source.at[peer]
            pltpu.make_async_remote_copy(
                src_ref=source, dst_ref=self.buffer.at[self.me],
                send_sem=self.send_sem, recv_sem=self.recv_sem,
                device_id=self.device(peer), device_id_type=MESH,
            ).start()

    def all_copies(self):
        part = self.buffer.at[pl.ds(0, self.count - 1)]
        return pltpu.make_async_remote_copy(
            src_ref=part, dst_ref=part, send_sem=self.send_sem, recv_sem=self.recv_sem,
            device_id=self.device(lax.rem(self.me + 1, self.count)), device_id_type=MESH,
        )

    def wait_recv(self):
        self.all_copies().wait_recv()

    def wait_send(self):
        self.all_copies().wait_send()

    def total(self):
        total = self.buffer[0]
        for i in range(1, self.count):
            total = total + self.buffer[i]
        return total


def body(
    sensor_count, slot_count,
    traffic, slot_in, day_in, sensor_out, slot_out, day_out,
    slot_ref, day_ref, t_win, t_high, t_low, w_cat, factor_sem, load_sem, round_sem,
    sensor_stage, slot_stage, day_stage, out_sem,
    win_sib, win_own, sib_recv, sib_ssem, sib_rsem, x_send, x_recv, x_ssem, x_rsem,
    gathered, gat_ssem, gat_rsem, fwd_ssem, fwd_rsem,
    c_wide, c_low,
    gram_part, gram_rows, gx_buf, gx_s, gx_r, gy_buf, gy_s, gy_r, gz_buf, gz_s, gz_r, ga_buf, ga_s, ga_r,
    slot_part, s8_buf, s8_s, s8_r, sz_buf, sz_s, sz_r, sa_buf, sa_s, sa_r, slot_all,
    con_part, con_rows, cy_buf, cy_s, cy_r, cz_buf, cz_s, cz_r, ca_buf, ca_s, ca_r, weights,
    dy_buf, dy_s, dy_r,
):
    days, slots, sensors = traffic.shape
    rows = days * slots
    padded = w_cat.shape[0]
    strips = NZ // days
    strip = slots // NY // strips
    own = sensors // GROUP
    sensor_index = lax.axis_index("sensor")
    slot_index = lax.axis_index("slot")
    day_index = lax.axis_index("day")
    z, y = lax.div(sensor_index, NY), lax.rem(sensor_index, NY)
    core = lax.rem(slot_index, 2)
    x_hi = lax.div(slot_index, 2)
    x = x_hi * 2 + day_index

    def device(z, y, x, core):
        return (z * NY + y, lax.div(x, 2) * 2 + core, lax.rem(x, 2))

    def chunk_of(x, core):
        return (lax.div(x, 2) * 2 + core) * 2 + lax.rem(x, 2)

    def group_device(index):
        return (sensor_index, lax.div(index, 2), lax.rem(index, 2))

    me = chunk_of(x, core)

    barrier = pltpu.get_barrier_semaphore()

    def greet(target):
        pl.semaphore_signal(barrier, inc=1, device_id=target, device_id_type=MESH)

    def greet_group(k, carry):
        greet(group_device(lax.rem(me + k, GROUP)))
        return carry

    lax.fori_loop(1, GROUP, greet_group, 0)
    for k in range(1, NY):
        greet(device(z, lax.rem(y + k, NY), x, core))
    for k in (1, NZ - 1):
        greet(device(lax.rem(z + k, NZ), y, x, core))
    barrier_count = (GROUP - 1) + (NY - 1) + 2

    def round_z(i):
        for k in (2**i, NZ - 2**i):
            target = device(lax.rem(z + k, NZ), y, x, core)
            pl.semaphore_signal(round_sem.at[i], inc=1, device_id=target, device_id_type=MESH)

    out_copies = [
        pltpu.make_async_copy(source, target, out_sem.at[i])
        for i, (source, target) in enumerate(((sensor_stage, sensor_out), (slot_stage, slot_out), (day_stage, day_out)))
    ]
    factor_loads = [
        pltpu.make_async_copy(slot_in, slot_ref, factor_sem.at[0]),
        pltpu.make_async_copy(day_in, day_ref, factor_sem.at[1]),
    ]
    for copy in factor_loads:
        copy.start()

    def target_x(j):
        return lax.rem(x + jnp.where(j == 0, 2, jnp.where(j == 1, 1, jnp.where(j == 2, 3, 0))), NX)

    def load_copy(chunk):
        lanes = pl.ds(pl.multiple_of(chunk * STRIDE, R), WINDOW)
        return pltpu.make_async_copy(traffic.at[:, :, lanes], t_win.at[chunk], load_sem.at[chunk])

    def load_step(j, carry):
        load_copy(chunk_of(target_x(j), 1 - core)).start()
        load_copy(chunk_of(target_x(j), core)).start()
        return carry

    lax.fori_loop(0, NX, load_step, 0)

    for c in range(GROUP):
        if c:
            gathered[c, 0 : SHIFT * c] = jnp.zeros((SHIFT * c, R), f32)
        if SHIFT * c + own < WINDOW:
            gathered[c, SHIFT * c + own :] = jnp.zeros((WINDOW - own - SHIFT * c, R), f32)
    c_wide[...] = jnp.zeros_like(c_wide)
    c_low[...] = jnp.zeros_like(c_low)
    for copy in factor_loads:
        copy.wait()

    slot_local = slot_ref[pl.ds(pl.multiple_of(slot_index * slots, 8), slots), :]
    khatri = [slot_local * day_ref[pl.ds(day_index * days + k, 1), :] for k in range(days)]
    khatri = jnp.concatenate(khatri + [jnp.zeros((padded - rows, R), f32)], axis=0)
    w_high, w_low = split(khatri)
    w_cat[:, 0:R] = w_high
    w_cat[:, R:] = w_low

    half = own // 2

    def rows_of(chunk):
        return pl.ds(pl.multiple_of(chunk * SHIFT, SHIFT), own)

    def half_rows_of(chunk, h):
        return pl.ds(pl.multiple_of(chunk * SHIFT + h * half, 8), half)

    def first_product(chunk, target):
        load_copy(chunk).wait()
        block = [t_win[chunk, k] for k in range(days)] + [jnp.zeros((padded - rows, WINDOW), f32)]
        high, low = split(jnp.concatenate(block, axis=0))
        t_high[chunk] = high
        t_low[chunk] = low
        wide = dot(high, w_cat[...], ((0,), (0,)))
        target[...] = wide[:, 0:R] + wide[:, R:] + dot(low, w_cat[:, 0:R], ((0,), (0,)))

    def sibling_copy(j):
        chunk = chunk_of(target_x(j), 1 - core)
        return pltpu.make_async_remote_copy(
            src_ref=win_sib.at[j].at[rows_of(chunk)], dst_ref=sib_recv.at[j],
            send_sem=sib_ssem.at[j], recv_sem=sib_rsem.at[j],
            device_id=device(z, y, x, 1 - core), device_id_type=MESH,
        )

    def x_copy(j, h):
        rows_h = pl.ds(pl.multiple_of(h * half, 8), half)
        return pltpu.make_async_remote_copy(
            src_ref=x_send.at[j].at[rows_h], dst_ref=x_recv.at[j].at[rows_h],
            send_sem=x_ssem.at[j, h], recv_sem=x_rsem.at[j, h],
            device_id=device(z, y, target_x(j), core), device_id_type=MESH,
        )

    def scatter_step(j, carry):
        @pl.when(j < NX)
        def _():
            first_product(chunk_of(target_x(j), 1 - core), win_sib.at[j])
            @pl.when(j == 0)
            def _():
                pl.semaphore_wait(barrier, barrier_count)
                round_z(0)

            sibling_copy(j).start()
            first_product(chunk_of(target_x(j), core), win_own.at[j])

        @pl.when(j > 0)
        def _():
            sibling_copy(j - 1).wait_recv()
            x_send[j - 1] = win_own[j - 1, rows_of(chunk_of(target_x(j - 1), core)), :] + sib_recv[j - 1]

            @pl.when(j < NX)
            def _():
                x_copy(j - 1, 0).start()

        return carry

    lax.fori_loop(0, NX + 1, scatter_step, 0)
    for j in range(NX - 1):
        x_copy(j, 1).start()

    pl.semaphore_wait(round_sem.at[0], 2)
    round_z(1)
    gram_day = gram_of(day_ref[...])
    inv_sensor = inverse(regularize(gram_of(slot_ref[...]) * gram_day))

    def own_half(h):
        total = x_send[NX - 1, h * half : (h + 1) * half]
        for j in range(NX - 1):
            x_copy(j, h).wait_recv()
            total = total + x_recv[j, h * half : (h + 1) * half]
        sensor_raw = dot(total, inv_sensor, precision=highest)
        gathered[me, half_rows_of(me, h), :] = sensor_raw
        return sensor_raw

    def device_y(p):
        return (z * NY + p, slot_index, day_index)

    def device_z(p):
        return (p * NY + y, slot_index, day_index)

    def device_32(p):
        return (z * NY + lax.div(p, 8), lax.rem(lax.div(p, 2), 4), lax.rem(p, 2))

    me_32 = y * 8 + me
    gx = Exchange((gx_buf, gx_s, gx_r), GROUP, me, group_device, gram_part)
    gy = Exchange((gy_buf, gy_s, gy_r), NY, y, device_y, gram_rows)
    gz = Exchange((gz_buf, gz_s, gz_r), NZ, z, device_z)
    ga = Exchange((ga_buf, ga_s, ga_r), 32, me_32, device_32)

    def source_x(j):
        return lax.rem(x + jnp.where(j == 0, 2, jnp.where(j == 1, 3, jnp.where(j == 2, 1, 0))), NX)

    def gather_copy(j, h, sender=False):
        chunk = me if sender else chunk_of(source_x(j), core)
        place = gathered.at[chunk].at[half_rows_of(chunk, h)]
        return pltpu.make_async_remote_copy(
            src_ref=place, dst_ref=place, send_sem=gat_ssem.at[j, h], recv_sem=gat_rsem.at[j, h],
            device_id=device(z, y, target_x(j), core), device_id_type=MESH,
        )

    def forward_copy(j, h, sender=False):
        chunk = chunk_of(source_x(j), core if sender else 1 - core)
        place = gathered.at[chunk].at[half_rows_of(chunk, h)]
        return pltpu.make_async_remote_copy(
            src_ref=place, dst_ref=place, send_sem=fwd_ssem.at[j, h], recv_sem=fwd_rsem.at[j, h],
            device_id=device(z, y, x, 1 - core), device_id_type=MESH,
        )

    def gather_start(h):
        for j in (1, 2, 0):
            gather_copy(j, h, True).start()
        forward_copy(3, h, True).start()

    pl.semaphore_wait(round_sem.at[1], 2)
    round_z(2)
    first_half = own_half(0)
    gather_start(0)
    gram = gram_of(first_half) + gram_of(own_half(1))
    for i in range(GROUP):
        gram_part[i] = gram[16 * i : 16 * i + 16]
    gx.start()
    gx_buf[me] = gram_part[me]
    gather_start(1)
    pl.semaphore_wait(round_sem.at[2], 2)

    def second_product(chunk):
        high, low = split(gathered[chunk])
        c_wide[...] += dot(t_high[chunk], jnp.concatenate([high, low], axis=1))
        c_low[...] += dot(t_low[chunk], high)

    def own_core(j):
        second_product(chunk_of(source_x(j), core))

    def other_core(j):
        forward_copy(j, 0).wait_recv()
        forward_copy(j, 1).wait_recv()
        second_product(chunk_of(source_x(j), 1 - core))

    def pass_on(j, h):
        gather_copy(j, h).wait_recv()
        forward_copy(j, h, True).start()

    def gather_step(i, carry):
        @pl.when(i == 0)
        def _():
            own_core(3)
            other_core(3)
            pass_on(1, 0)
            pass_on(2, 0)
            pass_on(0, 0)
            gx.wait_recv()
            gram = gx.total()
            for i in range(NY):
                gram_rows[i] = gram[4 * i : 4 * i + 4]
            gy.start()
            gy_buf[y] = gram_rows[y]
            pass_on(1, 1)
            pass_on(2, 1)

        @pl.when(i == 3)
        def _():
            pass_on(0, 1)

        j = jnp.where(i == 0, 1, jnp.where(i == 1, 2, 0))

        @pl.when(i != 2)
        def _():
            own_core(j)

        @pl.when(i == 2)
        def _():
            gy.wait_recv()
            gz_buf[z] = gy.total()
            gz.start()

        @pl.when(i >= 2)
        def _():
            other_core(jnp.where(i == 2, 1, 0))

        @pl.when(i == 2)
        def _():
            other_core(2)

        return carry

    lax.fori_loop(0, NX, gather_step, 0)

    contracted = c_wide[:, 0:R] + c_wide[:, R:] + c_low[...]
    contracted = [contracted[k * slots : (k + 1) * slots] for k in range(days)]
    part = contracted[0] * day_ref[pl.ds(day_index * days, 1), :]
    for k in range(1, days):
        part = part + contracted[k] * day_ref[pl.ds(day_index * days + k, 1), :]
    piece = slots // 8
    for i in range(8):
        slot_part[i] = part[i * piece : (i + 1) * piece]

    def device_8(p):
        return (z * NY + lax.div(p, 2), slot_index, lax.rem(p, 2))

    me_8 = y * 2 + day_index
    s8 = Exchange((s8_buf, s8_s, s8_r), 8, me_8, device_8, slot_part)
    sz = Exchange((sz_buf, sz_s, sz_r), NZ, z, device_z)
    sa = Exchange((sa_buf, sa_s, sa_r), 32, me_32, device_32)
    s8.start()
    s8_buf[me_8] = slot_part[me_8]

    for p in range(NY):
        for k in range(days):
            for m in range(strips):
                row = (p * strips + m) * strip
                con_part[p, k * strips + m] = contracted[k][row : row + strip]
        for i in range(days * strips, NZ):
            con_part[p, i] = jnp.zeros((strip, R), f32)
    cy = Exchange((cy_buf, cy_s, cy_r), NY, y, device_y, con_part)
    cz = Exchange((cz_buf, cz_s, cz_r), NZ, z, device_z, con_rows)
    ca = Exchange((ca_buf, ca_s, ca_r), NZ, z, device_z)
    cy.start()
    cy_buf[y] = con_part[y]

    for j in range(NX):
        sibling_copy(j).wait_send()
        for h in range(2):
            forward_copy(j, h, True).wait_send()
            if j < NX - 1:
                x_copy(j, h).wait_send()
                gather_copy(j, h, True).wait_send()
    gx.wait_send()
    gy.wait_send()

    s8.wait_recv()
    sz_buf[z] = s8.total()
    sz.start()

    cy.wait_recv()
    con_rows[...] = cy.total()
    cz.start()
    cz_buf[z] = con_rows[z]

    gz.wait_recv()
    ga_buf[me_32] = gz.total()
    ga.start()
    for exchange in (gz, s8, cy, sz):
        exchange.wait_send()
    sz.wait_recv()
    sa_buf[me_32] = sz.total()
    sa.start()
    ga.wait_recv()
    gram = jnp.concatenate([ga_buf[i * GROUP + g] for g in range(GROUP) for i in range(NY)], axis=0)

    def norms_of(gram, count):
        square = jnp.where(diagonal_mask(), gram, 0.0)
        row = jnp.sqrt(jnp.sum(square, axis=0, keepdims=True) / count + epsilon)
        column = jnp.sqrt(jnp.sum(square, axis=1, keepdims=True) / count + epsilon)
        return row, gram / (column * row)

    sensor_norms, gram_sensor = norms_of(gram, sensor_count)
    sensor_stage[...] = gathered[me, rows_of(me), :] / sensor_norms
    out_copies[0].start()
    cz.wait_recv()
    ca_buf[z] = cz.total()
    ca.start()
    inv_slot = inverse(regularize(gram_sensor * gram_day))

    ga.wait_send()
    cz.wait_send()
    sa.wait_recv()
    slot_rhs = [sa_buf[(i // 2) * 8 + s * 2 + i % 2] for s in range(4) for i in range(8)]
    slot_rhs = jnp.concatenate(slot_rhs, axis=0) / sensor_norms
    slot_all[...] = dot(slot_rhs, inv_slot, precision=highest)
    gram = gram_of(slot_all[...])
    slot_norms, gram_slot_new = norms_of(gram, slot_count)
    slot_new = slot_all[pl.ds(pl.multiple_of(slot_index * slots, 8), slots), :] / slot_norms
    slot_stage[...] = slot_new
    out_copies[1].start()

    weight = slot_new / sensor_norms
    for i in range(NY * strips):
        weights[i] = weight[i * strip : (i + 1) * strip]
    sa.wait_send()
    ca.wait_recv()
    for k in range(days):
        total = ca_buf[k * strips] * weights[y * strips]
        for m in range(1, strips):
            total = total + ca_buf[k * strips + m] * weights[y * strips + m]
        dy_buf[y * 4 + slot_index, k : k + 1] = jnp.sum(total, axis=0, keepdims=True)

    def device_16(p):
        return (z * NY + lax.div(p, 4), lax.rem(p, 4), day_index)

    me_16 = y * 4 + slot_index
    dy = Exchange((dy_buf, dy_s, dy_r), 16, me_16, device_16)
    dy.start()
    inv_day = inverse(regularize(gram_sensor * gram_slot_new))
    ca.wait_send()
    dy.wait_recv()
    day_stage[...] = dot(dy.total(), inv_day, precision=highest)
    out_copies[2].start()
    for copy in out_copies:
        copy.wait()

    dy.wait_send()


def on_device(traffic, slot_factor, day_factor):
    days, slots, sensors = traffic.shape
    slot_count = slot_factor.shape[0]
    sensor_count = sensors * lax.axis_size("sensor")
    own = sensors // GROUP
    padded = (days * slots + 15) // 16 * 16
    strip = slots // NY // (NZ // days)

    def exchange_scratch(count, *block):
        return [
            pltpu.VMEM((count, *block), f32),
            pltpu.SemaphoreType.DMA,
            pltpu.SemaphoreType.DMA,
        ]

    dma = pltpu.SemaphoreType.DMA
    scratch = [
        pltpu.VMEM(slot_factor.shape, f32),
        pltpu.VMEM(day_factor.shape, f32),
        pltpu.VMEM((GROUP, days, slots, WINDOW), f32),
        pltpu.VMEM((GROUP, padded, WINDOW), bf16),
        pltpu.VMEM((GROUP, padded, WINDOW), bf16),
        pltpu.VMEM((padded, 2 * R), bf16),
        dma((2,)),
        dma((GROUP,)),
        pltpu.SemaphoreType.REGULAR((3,)),
        pltpu.VMEM((own, R), f32),
        pltpu.VMEM((slots, R), f32),
        pltpu.VMEM((days, R), f32),
        dma((3,)),
        pltpu.VMEM((NX, WINDOW, R), f32),
        pltpu.VMEM((NX, WINDOW, R), f32),
        pltpu.VMEM((NX, own, R), f32),
        dma((NX,)), dma((NX,)),
        pltpu.VMEM((NX, own, R), f32),
        pltpu.VMEM((NX - 1, own, R), f32),
        dma((NX - 1, 2)), dma((NX - 1, 2)),
        pltpu.VMEM((GROUP, WINDOW, R), f32),
        dma((NX - 1, 2)), dma((NX - 1, 2)), dma((NX, 2)), dma((NX, 2)),
        pltpu.VMEM((padded, 2 * R), f32),
        pltpu.VMEM((padded, R), f32),
        pltpu.VMEM((GROUP, 16, R), f32),
        pltpu.VMEM((NY, 4, R), f32),
        *exchange_scratch(GROUP, 16, R),
        *exchange_scratch(NY, 4, R),
        *exchange_scratch(NZ, 4, R),
        *exchange_scratch(32, 4, R),
        pltpu.VMEM((8, slots // 8, R), f32),
        *exchange_scratch(8, slots // 8, R),
        *exchange_scratch(NZ, slots // 8, R),
        *exchange_scratch(32, slots // 8, R),
        pltpu.VMEM(slot_factor.shape, f32),
        pltpu.VMEM((NY, NZ, strip, R), f32),
        pltpu.VMEM((NZ, strip, R), f32),
        *exchange_scratch(NY, NZ, strip, R),
        *exchange_scratch(NZ, strip, R),
        *exchange_scratch(NZ, strip, R),
        pltpu.VMEM((slots // strip, strip, R), f32),
        *exchange_scratch(16, days, R),
    ]
    vmem = pl.BlockSpec(memory_space=pltpu.VMEM)

    def kernel(*refs):
        body(sensor_count, slot_count, *refs)

    results = pl.pallas_call(
        kernel,
        out_shape=(
            jax.ShapeDtypeStruct((own, R), f32),
            jax.ShapeDtypeStruct((slots, R), f32),
            jax.ShapeDtypeStruct((days, R), f32),
        ),
        in_specs=[pl.BlockSpec(memory_space=pltpu.HBM)] * 3,
        out_specs=(pl.BlockSpec(memory_space=pl.ANY),) * 3,
        scratch_shapes=scratch,
        compiler_params=pltpu.CompilerParams(
            collective_id=0, has_side_effects=True, vmem_limit_bytes=60 * 1024 * 1024
        ),
    )(traffic, slot_factor, day_factor)

    def store(*refs):
        for i in range(3):
            refs[3 + i][...] = refs[i][...]

    return pl.pallas_call(
        store,
        out_shape=tuple(jax.ShapeDtypeStruct(a.shape, f32) for a in results),
        in_specs=[vmem] * 3,
        out_specs=(vmem,) * 3,
    )(*results)


def solution(mesh):
    in_specs = (P("day", "slot", "sensor"), P(), P())
    out_specs = (P(("sensor", "slot", "day"), None), P("slot", None), P("day", None))
    return jax.shard_map(
        on_device, mesh=mesh, in_specs=in_specs, out_specs=out_specs, check_vma=False
    )
```

```python
import jax
import jax.numpy as jnp
from jax import lax
from jax.experimental import pallas as pl
from jax.experimental.pallas import tpu as pltpu
from jax.sharding import PartitionSpec as P

MESH = pl.DeviceIdType.MESH
highest = lax.Precision.HIGHEST
f32 = jnp.float32
bf16 = jnp.bfloat16
ridge_scale = 0.001
epsilon = 1e-05

R = 128
NX, NY, NZ = 4, 4, 16
GROUP = 8
WINDOW, STRIDE, SHIFT = 512, 384, 16


def dot(a, b, contract=((1,), (0,)), precision=None):
    return lax.dot_general(a, b, (contract, ((), ())), precision=precision, preferred_element_type=f32)


def gram_of(rows):
    return dot(rows, rows, ((0,), (0,)), highest)


def diagonal_mask():
    return lax.broadcasted_iota(jnp.int32, (R, R), 0) == lax.broadcasted_iota(jnp.int32, (R, R), 1)


def regularize(matrix):
    eye = diagonal_mask()
    mean = jnp.sum(jnp.where(eye, matrix, 0.0)) / R
    return matrix + jnp.where(eye, ridge_scale * mean, 0.0)


def inverse(matrix):
    lane = lax.broadcasted_iota(jnp.int32, (8, R), 1)
    sub = lax.broadcasted_iota(jnp.int32, (8, R), 0)
    lane_rest = lax.broadcasted_iota(jnp.int32, (R - 8, R), 1)

    def step(_, matrix):
        top, rest = matrix[0:8], matrix[8:]
        rows = [jnp.broadcast_to(top[i : i + 1, :], (8, R)) for i in range(8)]
        a = {(i, j): jnp.broadcast_to(rows[i][:, j : j + 1], (8, R)) for i in range(8) for j in range(i, 8)}
        rows = [jnp.where(lane == i, 1.0, jnp.where(lane < 8, 0.0, rows[i])) for i in range(8)]
        lower, scale = {}, []
        for t in range(8):
            scale.append(1.0 / a[t, t])
            for s in range(t + 1, 8):
                lower[s, t] = a[t, s] * scale[t]
            for s in range(t + 1, 8):
                for u in range(s, 8):
                    a[s, u] = a[s, u] - lower[s, t] * a[t, u]
                rows[s] = rows[s] - lower[s, t] * rows[t]
        rows = [rows[t] * scale[t] for t in range(8)]
        for t in range(7, -1, -1):
            for s in range(t):
                rows[s] = rows[s] - lower[t, s] * rows[t]
        new_top = rows[7]
        for i in range(7):
            new_top = jnp.where(sub == i, rows[i], new_top)
        base = jnp.where(lane_rest < 8, 0.0, rest)
        for i in range(8):
            base = base - rest[:, i : i + 1] * rows[i][0:1, :]
        return pltpu.roll(jnp.concatenate([base, new_top], axis=0), R - 8, 1)

    return lax.fori_loop(0, R // 8, step, matrix)


def split(value):
    high = value.astype(bf16)
    return high, (value - high.astype(f32)).astype(bf16)


class Exchange:
    def __init__(self, refs, count, me, device, source=None):
        self.buffer, self.send_sem, self.recv_sem = refs
        self.count, self.me, self.device, self.source = count, me, device, source

    def start(self):
        middle = self.count // 2
        for i in range(self.count - 1):
            k = middle + (i + 1) // 2 if i % 2 else middle - i // 2
            peer = lax.rem(self.me + k, self.count)
            source = self.buffer.at[self.me] if self.source is None else self.source.at[peer]
            pltpu.make_async_remote_copy(
                src_ref=source, dst_ref=self.buffer.at[self.me],
                send_sem=self.send_sem, recv_sem=self.recv_sem,
                device_id=self.device(peer), device_id_type=MESH,
            ).start()

    def all_copies(self):
        part = self.buffer.at[pl.ds(0, self.count - 1)]
        return pltpu.make_async_remote_copy(
            src_ref=part, dst_ref=part, send_sem=self.send_sem, recv_sem=self.recv_sem,
            device_id=self.device(lax.rem(self.me + 1, self.count)), device_id_type=MESH,
        )

    def wait_recv(self):
        self.all_copies().wait_recv()

    def wait_send(self):
        self.all_copies().wait_send()

    def total(self):
        total = self.buffer[0]
        for i in range(1, self.count):
            total = total + self.buffer[i]
        return total


def body(
    sensor_count, slot_count,
    traffic, slot_in, day_in, sensor_out, slot_out, day_out,
    slot_ref, day_ref, t_win, t_high, t_low, w_cat, factor_sem, load_sem, round_sem,
    sensor_stage, slot_stage, day_stage, out_sem,
    win_sib, win_own, sib_recv, sib_ssem, sib_rsem, x_send, x_recv, x_ssem, x_rsem,
    gathered, gat_ssem, gat_rsem, fwd_ssem, fwd_rsem,
    c_wide, c_low,
    gram_part, gram_rows, gx_buf, gx_s, gx_r, gy_buf, gy_s, gy_r, gz_buf, gz_s, gz_r, ga_buf, ga_s, ga_r,
    slot_part, s8_buf, s8_s, s8_r, sz_buf, sz_s, sz_r, sa_buf, sa_s, sa_r, slot_all,
    con_part, con_rows, cy_buf, cy_s, cy_r, cz_buf, cz_s, cz_r, ca_buf, ca_s, ca_r, weights,
    dy_buf, dy_s, dy_r,
):
    days, slots, sensors = traffic.shape
    rows = days * slots
    padded = w_cat.shape[0]
    strips = NZ // days
    strip = slots // NY // strips
    own = sensors // GROUP
    sensor_index = lax.axis_index("sensor")
    slot_index = lax.axis_index("slot")
    day_index = lax.axis_index("day")
    z, y = lax.div(sensor_index, NY), lax.rem(sensor_index, NY)
    core = lax.rem(slot_index, 2)
    x_hi = lax.div(slot_index, 2)
    x = x_hi * 2 + day_index

    def device(z, y, x, core):
        return (z * NY + y, lax.div(x, 2) * 2 + core, lax.rem(x, 2))

    def chunk_of(x, core):
        return (lax.div(x, 2) * 2 + core) * 2 + lax.rem(x, 2)

    def group_device(index):
        return (sensor_index, lax.div(index, 2), lax.rem(index, 2))

    me = chunk_of(x, core)

    barrier = pltpu.get_barrier_semaphore()

    def greet(target):
        pl.semaphore_signal(barrier, inc=1, device_id=target, device_id_type=MESH)

    def greet_group(k, carry):
        greet(group_device(lax.rem(me + k, GROUP)))
        return carry

    lax.fori_loop(1, GROUP, greet_group, 0)
    for k in range(1, NY):
        greet(device(z, lax.rem(y + k, NY), x, core))
    for k in (1, NZ - 1):
        greet(device(lax.rem(z + k, NZ), y, x, core))
    barrier_count = (GROUP - 1) + (NY - 1) + 2

    def round_z(i):
        for k in (2**i, NZ - 2**i):
            target = device(lax.rem(z + k, NZ), y, x, core)
            pl.semaphore_signal(round_sem.at[i], inc=1, device_id=target, device_id_type=MESH)

    out_copies = [
        pltpu.make_async_copy(source, target, out_sem.at[i])
        for i, (source, target) in enumerate(((sensor_stage, sensor_out), (slot_stage, slot_out), (day_stage, day_out)))
    ]
    factor_loads = [
        pltpu.make_async_copy(slot_in, slot_ref, factor_sem.at[0]),
        pltpu.make_async_copy(day_in, day_ref, factor_sem.at[1]),
    ]
    for copy in factor_loads:
        copy.start()

    def target_x(j):
        return lax.rem(x + jnp.where(j == 0, 2, jnp.where(j == 1, 1, jnp.where(j == 2, 3, 0))), NX)

    def load_copy(chunk):
        lanes = pl.ds(pl.multiple_of(chunk * STRIDE, R), WINDOW)
        return pltpu.make_async_copy(traffic.at[:, :, lanes], t_win.at[chunk], load_sem.at[chunk])

    def load_step(j, carry):
        load_copy(chunk_of(target_x(j), 1 - core)).start()
        load_copy(chunk_of(target_x(j), core)).start()
        return carry

    lax.fori_loop(0, NX, load_step, 0)

    for c in range(GROUP):
        if c:
            gathered[c, 0 : SHIFT * c] = jnp.zeros((SHIFT * c, R), f32)
        if SHIFT * c + own < WINDOW:
            gathered[c, SHIFT * c + own :] = jnp.zeros((WINDOW - own - SHIFT * c, R), f32)
    c_wide[...] = jnp.zeros_like(c_wide)
    c_low[...] = jnp.zeros_like(c_low)
    for copy in factor_loads:
        copy.wait()

    slot_local = slot_ref[pl.ds(pl.multiple_of(slot_index * slots, 8), slots), :]
    khatri = [slot_local * day_ref[pl.ds(day_index * days + k, 1), :] for k in range(days)]
    khatri = jnp.concatenate(khatri + [jnp.zeros((padded - rows, R), f32)], axis=0)
    w_high, w_low = split(khatri)
    w_cat[:, 0:R] = w_high
    w_cat[:, R:] = w_low

    half = own // 2

    def rows_of(chunk):
        return pl.ds(pl.multiple_of(chunk * SHIFT, SHIFT), own)

    def half_rows_of(chunk, h):
        return pl.ds(pl.multiple_of(chunk * SHIFT + h * half, 8), half)

    def first_product(chunk, target):
        load_copy(chunk).wait()
        block = [t_win[chunk, k] for k in range(days)] + [jnp.zeros((padded - rows, WINDOW), f32)]
        high, low = split(jnp.concatenate(block, axis=0))
        t_high[chunk] = high
        t_low[chunk] = low
        wide = dot(high, w_cat[...], ((0,), (0,)))
        target[...] = wide[:, 0:R] + wide[:, R:] + dot(low, w_cat[:, 0:R], ((0,), (0,)))

    def sibling_copy(j):
        chunk = chunk_of(target_x(j), 1 - core)
        return pltpu.make_async_remote_copy(
            src_ref=win_sib.at[j].at[rows_of(chunk)], dst_ref=sib_recv.at[j],
            send_sem=sib_ssem.at[j], recv_sem=sib_rsem.at[j],
            device_id=device(z, y, x, 1 - core), device_id_type=MESH,
        )

    def x_copy(j, h):
        rows_h = pl.ds(pl.multiple_of(h * half, 8), half)
        return pltpu.make_async_remote_copy(
            src_ref=x_send.at[j].at[rows_h], dst_ref=x_recv.at[j].at[rows_h],
            send_sem=x_ssem.at[j, h], recv_sem=x_rsem.at[j, h],
            device_id=device(z, y, target_x(j), core), device_id_type=MESH,
        )

    def scatter_step(j, carry):
        @pl.when(j < NX)
        def _():
            first_product(chunk_of(target_x(j), 1 - core), win_sib.at[j])
            @pl.when(j == 0)
            def _():
                pl.semaphore_wait(barrier, barrier_count)
                round_z(0)

            sibling_copy(j).start()
            first_product(chunk_of(target_x(j), core), win_own.at[j])

        @pl.when(j > 0)
        def _():
            sibling_copy(j - 1).wait_recv()
            x_send[j - 1] = win_own[j - 1, rows_of(chunk_of(target_x(j - 1), core)), :] + sib_recv[j - 1]

            @pl.when(j < NX)
            def _():
                x_copy(j - 1, 0).start()

        return carry

    lax.fori_loop(0, NX + 1, scatter_step, 0)
    for j in range(NX - 1):
        x_copy(j, 1).start()

    pl.semaphore_wait(round_sem.at[0], 2)
    round_z(1)
    gram_day = gram_of(day_ref[...])
    inv_sensor = inverse(regularize(gram_of(slot_ref[...]) * gram_day))

    def own_half(h):
        total = x_send[NX - 1, h * half : (h + 1) * half]
        for j in range(NX - 1):
            x_copy(j, h).wait_recv()
            total = total + x_recv[j, h * half : (h + 1) * half]
        sensor_raw = dot(total, inv_sensor, precision=highest)
        gathered[me, half_rows_of(me, h), :] = sensor_raw
        return sensor_raw

    def device_y(p):
        return (z * NY + p, slot_index, day_index)

    def device_z(p):
        return (p * NY + y, slot_index, day_index)

    def device_32(p):
        return (z * NY + lax.div(p, 8), lax.rem(lax.div(p, 2), 4), lax.rem(p, 2))

    me_32 = y * 8 + me
    gx = Exchange((gx_buf, gx_s, gx_r), GROUP, me, group_device, gram_part)
    gy = Exchange((gy_buf, gy_s, gy_r), NY, y, device_y, gram_rows)
    gz = Exchange((gz_buf, gz_s, gz_r), NZ, z, device_z)
    ga = Exchange((ga_buf, ga_s, ga_r), 32, me_32, device_32)

    def source_x(j):
        return lax.rem(x + jnp.where(j == 0, 2, jnp.where(j == 1, 3, jnp.where(j == 2, 1, 0))), NX)

    def gather_copy(j, h, sender=False):
        chunk = me if sender else chunk_of(source_x(j), core)
        place = gathered.at[chunk].at[half_rows_of(chunk, h)]
        return pltpu.make_async_remote_copy(
            src_ref=place, dst_ref=place, send_sem=gat_ssem.at[j, h], recv_sem=gat_rsem.at[j, h],
            device_id=device(z, y, target_x(j), core), device_id_type=MESH,
        )

    def forward_copy(j, h, sender=False):
        chunk = chunk_of(source_x(j), core if sender else 1 - core)
        place = gathered.at[chunk].at[half_rows_of(chunk, h)]
        return pltpu.make_async_remote_copy(
            src_ref=place, dst_ref=place, send_sem=fwd_ssem.at[j, h], recv_sem=fwd_rsem.at[j, h],
            device_id=device(z, y, x, 1 - core), device_id_type=MESH,
        )

    def gather_start(h):
        for j in (1, 2, 0):
            gather_copy(j, h, True).start()
        forward_copy(3, h, True).start()

    pl.semaphore_wait(round_sem.at[1], 2)
    round_z(2)
    first_half = own_half(0)
    gather_start(0)
    gram = gram_of(first_half) + gram_of(own_half(1))
    for i in range(GROUP):
        gram_part[i] = gram[16 * i : 16 * i + 16]
    gx.start()
    gx_buf[me] = gram_part[me]
    gather_start(1)
    pl.semaphore_wait(round_sem.at[2], 2)

    def second_product(chunk):
        high, low = split(gathered[chunk])
        c_wide[...] += dot(t_high[chunk], jnp.concatenate([high, low], axis=1))
        c_low[...] += dot(t_low[chunk], high)

    def own_core(j):
        second_product(chunk_of(source_x(j), core))

    def other_core(j):
        forward_copy(j, 0).wait_recv()
        forward_copy(j, 1).wait_recv()
        second_product(chunk_of(source_x(j), 1 - core))

    def pass_on(j, h):
        gather_copy(j, h).wait_recv()
        forward_copy(j, h, True).start()

    def gather_step(i, carry):
        @pl.when(i == 0)
        def _():
            own_core(3)
            other_core(3)
            pass_on(1, 0)
            pass_on(2, 0)
            pass_on(0, 0)
            gx.wait_recv()
            gram = gx.total()
            for i in range(NY):
                gram_rows[i] = gram[4 * i : 4 * i + 4]
            gy.start()
            gy_buf[y] = gram_rows[y]
            pass_on(1, 1)
            pass_on(2, 1)

        @pl.when(i == 3)
        def _():
            pass_on(0, 1)

        j = jnp.where(i == 0, 1, jnp.where(i == 1, 2, 0))

        @pl.when(i != 2)
        def _():
            own_core(j)

        @pl.when(i == 2)
        def _():
            gy.wait_recv()
            gz_buf[z] = gy.total()
            gz.start()

        @pl.when(i >= 2)
        def _():
            other_core(jnp.where(i == 2, 1, 0))

        @pl.when(i == 2)
        def _():
            other_core(2)

        return carry

    lax.fori_loop(0, NX, gather_step, 0)

    contracted = c_wide[:, 0:R] + c_wide[:, R:] + c_low[...]
    contracted = [contracted[k * slots : (k + 1) * slots] for k in range(days)]
    part = contracted[0] * day_ref[pl.ds(day_index * days, 1), :]
    for k in range(1, days):
        part = part + contracted[k] * day_ref[pl.ds(day_index * days + k, 1), :]
    piece = slots // 8
    for i in range(8):
        slot_part[i] = part[i * piece : (i + 1) * piece]

    def device_8(p):
        return (z * NY + lax.div(p, 2), slot_index, lax.rem(p, 2))

    me_8 = y * 2 + day_index
    s8 = Exchange((s8_buf, s8_s, s8_r), 8, me_8, device_8, slot_part)
    sz = Exchange((sz_buf, sz_s, sz_r), NZ, z, device_z)
    sa = Exchange((sa_buf, sa_s, sa_r), 32, me_32, device_32)
    s8.start()
    s8_buf[me_8] = slot_part[me_8]

    for p in range(NY):
        for k in range(days):
            for m in range(strips):
                row = (p * strips + m) * strip
                con_part[p, k * strips + m] = contracted[k][row : row + strip]
        for i in range(days * strips, NZ):
            con_part[p, i] = jnp.zeros((strip, R), f32)
    cy = Exchange((cy_buf, cy_s, cy_r), NY, y, device_y, con_part)
    cz = Exchange((cz_buf, cz_s, cz_r), NZ, z, device_z, con_rows)
    ca = Exchange((ca_buf, ca_s, ca_r), NZ, z, device_z)
    cy.start()
    cy_buf[y] = con_part[y]

    for j in range(NX):
        sibling_copy(j).wait_send()
        for h in range(2):
            forward_copy(j, h, True).wait_send()
            if j < NX - 1:
                x_copy(j, h).wait_send()
                gather_copy(j, h, True).wait_send()
    gx.wait_send()
    gy.wait_send()

    s8.wait_recv()
    sz_buf[z] = s8.total()
    sz.start()
    gz.wait_recv()
    ga_buf[me_32] = gz.total()
    ga.start()

    cy.wait_recv()
    con_rows[...] = cy.total()
    cz.start()
    cz_buf[z] = con_rows[z]

    for exchange in (gz, s8, cy, sz):
        exchange.wait_send()
    sz.wait_recv()
    sa_buf[me_32] = sz.total()
    sa.start()
    ga.wait_recv()
    gram = jnp.concatenate([ga_buf[i * GROUP + g] for g in range(GROUP) for i in range(NY)], axis=0)

    def norms_of(gram, count):
        square = jnp.where(diagonal_mask(), gram, 0.0)
        row = jnp.sqrt(jnp.sum(square, axis=0, keepdims=True) / count + epsilon)
        column = jnp.sqrt(jnp.sum(square, axis=1, keepdims=True) / count + epsilon)
        return row, gram / (column * row)

    sensor_norms, gram_sensor = norms_of(gram, sensor_count)
    sensor_stage[...] = gathered[me, rows_of(me), :] / sensor_norms
    out_copies[0].start()
    cz.wait_recv()
    ca_buf[z] = cz.total()
    ca.start()
    inv_slot = inverse(regularize(gram_sensor * gram_day))

    ga.wait_send()
    cz.wait_send()
    sa.wait_recv()
    slot_rhs = [sa_buf[(i // 2) * 8 + s * 2 + i % 2] for s in range(4) for i in range(8)]
    slot_rhs = jnp.concatenate(slot_rhs, axis=0) / sensor_norms
    slot_all[...] = dot(slot_rhs, inv_slot, precision=highest)
    gram = gram_of(slot_all[...])
    slot_norms, gram_slot_new = norms_of(gram, slot_count)
    slot_new = slot_all[pl.ds(pl.multiple_of(slot_index * slots, 8), slots), :] / slot_norms
    slot_stage[...] = slot_new
    out_copies[1].start()

    weight = slot_new / sensor_norms
    for i in range(NY * strips):
        weights[i] = weight[i * strip : (i + 1) * strip]
    sa.wait_send()
    ca.wait_recv()
    for k in range(days):
        total = ca_buf[k * strips] * weights[y * strips]
        for m in range(1, strips):
            total = total + ca_buf[k * strips + m] * weights[y * strips + m]
        dy_buf[y * 4 + slot_index, k : k + 1] = jnp.sum(total, axis=0, keepdims=True)

    def device_16(p):
        return (z * NY + lax.div(p, 4), lax.rem(p, 4), day_index)

    me_16 = y * 4 + slot_index
    dy = Exchange((dy_buf, dy_s, dy_r), 16, me_16, device_16)
    dy.start()
    inv_day = inverse(regularize(gram_sensor * gram_slot_new))
    ca.wait_send()
    dy.wait_recv()
    day_stage[...] = dot(dy.total(), inv_day, precision=highest)
    out_copies[2].start()
    for copy in out_copies:
        copy.wait()

    dy.wait_send()


def on_device(traffic, slot_factor, day_factor):
    days, slots, sensors = traffic.shape
    slot_count = slot_factor.shape[0]
    sensor_count = sensors * lax.axis_size("sensor")
    own = sensors // GROUP
    padded = (days * slots + 15) // 16 * 16
    strip = slots // NY // (NZ // days)

    def exchange_scratch(count, *block):
        return [
            pltpu.VMEM((count, *block), f32),
            pltpu.SemaphoreType.DMA,
            pltpu.SemaphoreType.DMA,
        ]

    dma = pltpu.SemaphoreType.DMA
    scratch = [
        pltpu.VMEM(slot_factor.shape, f32),
        pltpu.VMEM(day_factor.shape, f32),
        pltpu.VMEM((GROUP, days, slots, WINDOW), f32),
        pltpu.VMEM((GROUP, padded, WINDOW), bf16),
        pltpu.VMEM((GROUP, padded, WINDOW), bf16),
        pltpu.VMEM((padded, 2 * R), bf16),
        dma((2,)),
        dma((GROUP,)),
        pltpu.SemaphoreType.REGULAR((3,)),
        pltpu.VMEM((own, R), f32),
        pltpu.VMEM((slots, R), f32),
        pltpu.VMEM((days, R), f32),
        dma((3,)),
        pltpu.VMEM((NX, WINDOW, R), f32),
        pltpu.VMEM((NX, WINDOW, R), f32),
        pltpu.VMEM((NX, own, R), f32),
        dma((NX,)), dma((NX,)),
        pltpu.VMEM((NX, own, R), f32),
        pltpu.VMEM((NX - 1, own, R), f32),
        dma((NX - 1, 2)), dma((NX - 1, 2)),
        pltpu.VMEM((GROUP, WINDOW, R), f32),
        dma((NX - 1, 2)), dma((NX - 1, 2)), dma((NX, 2)), dma((NX, 2)),
        pltpu.VMEM((padded, 2 * R), f32),
        pltpu.VMEM((padded, R), f32),
        pltpu.VMEM((GROUP, 16, R), f32),
        pltpu.VMEM((NY, 4, R), f32),
        *exchange_scratch(GROUP, 16, R),
        *exchange_scratch(NY, 4, R),
        *exchange_scratch(NZ, 4, R),
        *exchange_scratch(32, 4, R),
        pltpu.VMEM((8, slots // 8, R), f32),
        *exchange_scratch(8, slots // 8, R),
        *exchange_scratch(NZ, slots // 8, R),
        *exchange_scratch(32, slots // 8, R),
        pltpu.VMEM(slot_factor.shape, f32),
        pltpu.VMEM((NY, NZ, strip, R), f32),
        pltpu.VMEM((NZ, strip, R), f32),
        *exchange_scratch(NY, NZ, strip, R),
        *exchange_scratch(NZ, strip, R),
        *exchange_scratch(NZ, strip, R),
        pltpu.VMEM((slots // strip, strip, R), f32),
        *exchange_scratch(16, days, R),
    ]
    vmem = pl.BlockSpec(memory_space=pltpu.VMEM)

    def kernel(*refs):
        body(sensor_count, slot_count, *refs)

    results = pl.pallas_call(
        kernel,
        out_shape=(
            jax.ShapeDtypeStruct((own, R), f32),
            jax.ShapeDtypeStruct((slots, R), f32),
            jax.ShapeDtypeStruct((days, R), f32),
        ),
        in_specs=[pl.BlockSpec(memory_space=pltpu.HBM)] * 3,
        out_specs=(pl.BlockSpec(memory_space=pl.ANY),) * 3,
        scratch_shapes=scratch,
        compiler_params=pltpu.CompilerParams(
            collective_id=0, has_side_effects=True, vmem_limit_bytes=60 * 1024 * 1024
        ),
    )(traffic, slot_factor, day_factor)

    def store(*refs):
        for i in range(3):
            refs[3 + i][...] = refs[i][...]

    return pl.pallas_call(
        store,
        out_shape=tuple(jax.ShapeDtypeStruct(a.shape, f32) for a in results),
        in_specs=[vmem] * 3,
        out_specs=(vmem,) * 3,
    )(*results)


def solution(mesh):
    in_specs = (P("day", "slot", "sensor"), P(), P())
    out_specs = (P(("sensor", "slot", "day"), None), P("slot", None), P("day", None))
    return jax.shard_map(
        on_device, mesh=mesh, in_specs=in_specs, out_specs=out_specs, check_vma=False
    )
```
